256 devices in a mesh: ctx: 8 (over z_hi, x), tp: 4 (over z_lo), dec: 8 (over y, core).
Axes of the slice: x: 4, y: 4, z: 8 (z_hi: 2, z_lo: 4; z = z_hi * 4 + z_lo), core: 2. Of those that a mesh axis runs over, the one named last changes fastest.
Arguments:
- stretch_query_rows: bfloat16 [2048, 8192], P('ctx', 'tp'), may hold values from -14 to 14
- stretch_key_rows: bfloat16 [2048, 1024], P('ctx', 'tp'), may hold values from -6 to 6
- stretch_value_rows: bfloat16 [2048, 1024], P('ctx', 'tp'), may hold values from -5 to 5
- prefix_key_rows: bfloat16 [32768, 1024], P(('ctx', 'dec'), 'tp'), may hold values from -12 to 12
- prefix_value_rows: bfloat16 [32768, 1024], P(('ctx', 'dec'), 'tp'), may hold values from -5 to 5
- offset: int32 [1], replicated, may hold values from 8192 to 32768
- decode_query_rows: bfloat16 [2, 128, 8, 1024], P(None, ('ctx', 'tp'), 'dec'), may hold values from -21 to 21
- decode_keys: bfloat16 [2, 128, 8, 128], P(None, ('ctx', 'tp'), 'dec'), may hold values from -13 to 13
- decode_value_rows: bfloat16 [2, 128, 8, 128], P(None, ('ctx', 'tp'), 'dec'), may hold values from -5 to 5
- cache_keys: bfloat16 [128, 8, 2048, 128], P(('ctx', 'tp'), 'dec'), may hold values from -12 to 12
- cached_value_rows: bfloat16 [128, 8, 2048, 128], P(('ctx', 'tp'), 'dec'), may hold values from -5 to 5
- cache_lengths: int32 [128], P(('ctx', 'tp')), may hold values from 2 to 2048, as said below
- head_slot_index: int32 [8], replicated, may hold values from 0 to 7, each once
Outputs:
- prefill_out: bfloat16 [2048, 8192], P(('ctx', 'dec'), 'tp')
- decode_output: bfloat16 [2, 128, 8, 1024], P(None, ('ctx', 'tp'), 'dec')
The draws below stay inside these ranges and needn't reach their ends.
Inputs may be any that keep to these rules, and one draw needn't show every extreme that they name: `cache_lengths`: 2048 and 2 are each taken by some request in every draw. `head_slot_index`: each slot holds one head.
All inputs are finite; a program needn't handle non-finite values.
Results may differ from the reference program's by a relative error of at most 0.0012.
Values may be sent and summed in bfloat16 or wider, within the bound.
A program may use at most 256 MiB of HBM per device.

```python
import math
import jax
import jax.numpy as jnp
from jax import lax

HQ = 64
KEY_VALUE_HEADS = 8
HEAD_SIZE = 128
QUERY_GROUP = 8
STRETCH_LENGTH = 2048
PREFIX_LENGTH = 32768
DECODE_ROWS = 128
CACHE_SLOTS = 2048
DECODE_STEPS = 2


def sign_matrix(key, array_shape):
    return jnp.where(jax.random.bernoulli(key, 0.5, array_shape), 1.0, -1.0).astype(jnp.float32)


def head_directions(key):
    return sign_matrix(jax.random.fold_in(key, 101), (KEY_VALUE_HEADS, HEAD_SIZE))


def own_direction(key):
    return jnp.clip(jax.random.normal(jax.random.fold_in(key, 103), (DECODE_STEPS, DECODE_ROWS, KEY_VALUE_HEADS, HEAD_SIZE), jnp.float32), -5.0, 5.0)


def draw_stretch_query_rows(key, part):
    shared_part = head_directions(key)
    key = jax.random.fold_in(key, 1)
    jitter_key = jax.random.fold_in(key, 0)
    array_shape = (STRETCH_LENGTH, KEY_VALUE_HEADS, QUERY_GROUP, HEAD_SIZE)
    random_noise = jnp.clip(jax.random.normal(jitter_key, array_shape, jnp.float32), -5.0, 5.0)
    increment_size = (2.0 / math.sqrt(HEAD_SIZE)) ** 0.5
    final_output = 2.5 * random_noise + increment_size * shared_part[None, :, None, :]
    return final_output.reshape(STRETCH_LENGTH, HQ * HEAD_SIZE).astype(jnp.bfloat16)


def draw_stretch_key_rows(key, part):
    shared_part = head_directions(key)
    key = jax.random.fold_in(key, 3)
    array_shape = (STRETCH_LENGTH, KEY_VALUE_HEADS, HEAD_SIZE)
    random_noise = jnp.clip(jax.random.normal(key, array_shape, jnp.float32), -5.0, 5.0)
    increment_size = (2.0 / math.sqrt(HEAD_SIZE)) ** 0.5
    return (random_noise + increment_size * shared_part[None, :, :]).reshape(STRETCH_LENGTH, KEY_VALUE_HEADS * HEAD_SIZE).astype(jnp.bfloat16)


def draw_prefix_key_rows(key, part):
    key = jax.random.fold_in(key, 2)
    jitter_key = jax.random.fold_in(key, 0)
    array_shape = (PREFIX_LENGTH, KEY_VALUE_HEADS, HEAD_SIZE)
    random_noise = jnp.clip(jax.random.normal(jitter_key, array_shape, jnp.float32), -5.0, 5.0)
    return random_noise.reshape(PREFIX_LENGTH, KEY_VALUE_HEADS * HEAD_SIZE).astype(jnp.bfloat16)


def draw_decode_query_rows(key, part):
    shared_part = own_direction(key)
    key = jax.random.fold_in(key, 4)
    jitter_key = jax.random.fold_in(key, 0)
    array_shape = (DECODE_STEPS, DECODE_ROWS, KEY_VALUE_HEADS, QUERY_GROUP, HEAD_SIZE)
    random_noise = jnp.clip(jax.random.normal(jitter_key, array_shape, jnp.float32), -5.0, 5.0)
    lift_size = (9.0 / math.sqrt(HEAD_SIZE)) ** 0.5
    final_output = 2.5 * random_noise + lift_size * shared_part[:, :, :, None, :]
    return final_output.reshape(DECODE_STEPS, DECODE_ROWS, KEY_VALUE_HEADS, QUERY_GROUP * HEAD_SIZE).astype(jnp.bfloat16)


def draw_decode_keys(key, part):
    shared_part = own_direction(key)
    key = jax.random.fold_in(key, 5)
    array_shape = (DECODE_STEPS, DECODE_ROWS, KEY_VALUE_HEADS, HEAD_SIZE)
    random_noise = jnp.clip(jax.random.normal(key, array_shape, jnp.float32), -5.0, 5.0)
    lift_size = (9.0 / math.sqrt(HEAD_SIZE)) ** 0.5
    return (random_noise + lift_size * shared_part).astype(jnp.bfloat16)


def draw_cache_keys(key, part):
    key = jax.random.fold_in(key, 6)
    array_shape = (DECODE_ROWS, KEY_VALUE_HEADS, CACHE_SLOTS, HEAD_SIZE)
    random_noise = jnp.clip(jax.random.normal(key, array_shape, jnp.float32), -5.0, 5.0)
    return random_noise.astype(jnp.bfloat16)


def draw_cache_lengths(key, part):
    key = jax.random.fold_in(key, 7)
    len_key, top_key, low_key = jax.random.split(key, 3)
    lengths = jax.random.randint(len_key, (DECODE_ROWS,), 2, CACHE_SLOTS + 1)
    longest = jax.random.randint(top_key, (), 0, DECODE_ROWS)
    shortest = (longest + 1 + jax.random.randint(low_key, (), 0, DECODE_ROWS - 1)) % DECODE_ROWS
    row_ids = jnp.arange(DECODE_ROWS)
    lengths = jnp.where(row_ids == longest, CACHE_SLOTS, lengths)
    return jnp.where(row_ids == shortest, 2, lengths).astype(jnp.int32)


def block_levels(rng, shape, cuts, smallest, largest):
    factor_of, own = 1.0, jax.random.fold_in(rng, 6)
    for axis_at, shards_of in cuts:
        steps = jnp.exp(jax.random.uniform(jax.random.fold_in(own, axis_at), (shards_of,), jnp.float32, smallest / len(cuts), largest / len(cuts)))
        factor_of = factor_of * jnp.repeat(steps, shape[axis_at] // shards_of).reshape([-1 if axis == axis_at else 1 for axis in range(len(shape))])
    return factor_of


def gaussian(rng, dims, deviation, reach, shards=(), kind=jnp.bfloat16):
    values = deviation * jax.random.normal(rng, dims, jnp.float32)
    if shards:
        values = values * block_levels(rng, dims, shards, -0.22, 0.18)
    return jnp.clip(values, -reach, reach).astype(kind)


def setup_inputs(seed: int = 0) -> dict:
    keys = jax.random.split(jax.random.key(seed), 14)
    stretch_query_rows = draw_stretch_query_rows(jax.random.fold_in(keys[13], 71), 0)
    stretch_key_rows = draw_stretch_key_rows(jax.random.fold_in(keys[13], 71), 0)
    stretch_value_rows = gaussian(keys[2], (STRETCH_LENGTH, KEY_VALUE_HEADS * HEAD_SIZE), 1.0, 5.0, ((0, 8), (1, 4)))
    prefix_key_rows = draw_prefix_key_rows(jax.random.fold_in(keys[13], 71), 0)
    prefix_value_rows = gaussian(keys[4], (PREFIX_LENGTH, KEY_VALUE_HEADS * HEAD_SIZE), 1.0, 5.0, ((0, 64), (1, 4)))
    offset = jax.random.randint(keys[5], (1,), PREFIX_LENGTH // 4, PREFIX_LENGTH + 1).astype(jnp.int32)
    decode_query_rows = draw_decode_query_rows(jax.random.fold_in(keys[13], 71), 0)
    decode_keys = draw_decode_keys(jax.random.fold_in(keys[13], 71), 0)
    decode_value_rows = gaussian(keys[8], (DECODE_STEPS, DECODE_ROWS, KEY_VALUE_HEADS, HEAD_SIZE), 1.0, 5.0, ((1, 32), (2, 8)))
    cache_keys = draw_cache_keys(jax.random.fold_in(keys[13], 71), 0)
    cached_value_rows = gaussian(keys[10], (DECODE_ROWS, KEY_VALUE_HEADS, CACHE_SLOTS, HEAD_SIZE), 1.0, 5.0, ((0, 32), (1, 8)))
    cache_lengths = draw_cache_lengths(jax.random.fold_in(keys[13], 71), 0)
    head_slot_index = jax.random.permutation(keys[12], KEY_VALUE_HEADS).astype(jnp.int32)
    return dict(stretch_query_rows=stretch_query_rows, stretch_key_rows=stretch_key_rows, stretch_value_rows=stretch_value_rows, prefix_key_rows=prefix_key_rows, prefix_value_rows=prefix_value_rows, offset=offset, decode_query_rows=decode_query_rows, decode_keys=decode_keys, decode_value_rows=decode_value_rows, cache_keys=cache_keys, cached_value_rows=cached_value_rows, cache_lengths=cache_lengths, head_slot_index=head_slot_index)


masked_score = -1.0e30


def reference(stretch_query_rows, stretch_key_rows, stretch_value_rows, prefix_key_rows, prefix_value_rows, offset, decode_query_rows, decode_keys, decode_value_rows, cache_keys, cached_value_rows, cache_lengths, head_slot_index):
    scaling = HEAD_SIZE ** -0.5
    row_block_index = min(256, STRETCH_LENGTH)
    number_blocks = STRETCH_LENGTH // row_block_index
    total_length = PREFIX_LENGTH + STRETCH_LENGTH
    combined_keys = jnp.concatenate([prefix_key_rows, stretch_key_rows], axis=0).reshape(total_length, KEY_VALUE_HEADS, HEAD_SIZE)
    combined_values = jnp.concatenate([prefix_value_rows, stretch_value_rows], axis=0).reshape(total_length, KEY_VALUE_HEADS, HEAD_SIZE)
    query_rows = stretch_query_rows.reshape(STRETCH_LENGTH, KEY_VALUE_HEADS, QUERY_GROUP, HEAD_SIZE)
    key_index = jnp.arange(total_length, dtype=jnp.int32)
    prompt_end = offset[0]

    def head_block(ids):
        head_id, block_id = ids
        head_queries = lax.dynamic_index_in_dim(query_rows, head_id, 1, keepdims=False)
        block_queries = lax.dynamic_slice_in_dim(head_queries, block_id * row_block_index, row_block_index, 0)
        head_keys = lax.dynamic_index_in_dim(combined_keys, head_id, 1, keepdims=False)
        head_values = lax.dynamic_index_in_dim(combined_values, head_id, 1, keepdims=False)
        scores = jnp.einsum("rgd,kd->rgk", block_queries.astype(jnp.float32), head_keys.astype(jnp.float32)) * scaling
        row_index = block_id * row_block_index + jnp.arange(row_block_index, dtype=jnp.int32)
        usable = jnp.where(key_index[None, :] < PREFIX_LENGTH, key_index[None, :] < prompt_end, key_index[None, :] - PREFIX_LENGTH <= row_index[:, None])
        scores = jnp.where(usable[:, None, :], scores, masked_score)
        row_max = jnp.max(scores, axis=-1, keepdims=True)
        weights = jnp.where(usable[:, None, :], jnp.exp(scores - row_max), 0.0)
        mixed = jnp.einsum("rgk,kd->rgd", weights, head_values.astype(jnp.float32), precision=lax.Precision.HIGHEST)
        return mixed / jnp.sum(weights, axis=-1)[..., None]

    head_numbers = jnp.repeat(jnp.arange(KEY_VALUE_HEADS, dtype=jnp.int32), number_blocks)
    block_numbers = jnp.tile(jnp.arange(number_blocks, dtype=jnp.int32), KEY_VALUE_HEADS)
    block_list = lax.map(head_block, (head_numbers, block_numbers))
    block_list = block_list.reshape(KEY_VALUE_HEADS, number_blocks, row_block_index, QUERY_GROUP, HEAD_SIZE).transpose(1, 2, 0, 3, 4)
    prefill_out = block_list.reshape(STRETCH_LENGTH, HQ * HEAD_SIZE).astype(jnp.bfloat16)

    slot_head_index = jnp.zeros((KEY_VALUE_HEADS,), jnp.int32).at[head_slot_index].set(jnp.arange(KEY_VALUE_HEADS, dtype=jnp.int32))
    slot_key_rows = jnp.take(stretch_key_rows.reshape(STRETCH_LENGTH, KEY_VALUE_HEADS, HEAD_SIZE), slot_head_index, axis=1)
    slot_value_rows = jnp.take(stretch_value_rows.reshape(STRETCH_LENGTH, KEY_VALUE_HEADS, HEAD_SIZE), slot_head_index, axis=1)
    step_index = jnp.arange(DECODE_STEPS, dtype=jnp.int32)
    cache_index = jnp.arange(CACHE_SLOTS, dtype=jnp.int32)

    def decode_row(row_number):
        row_query_matrix = lax.dynamic_index_in_dim(decode_query_rows, row_number, 1, keepdims=False).reshape(DECODE_STEPS, KEY_VALUE_HEADS, QUERY_GROUP, HEAD_SIZE)
        row_cache_keys = lax.dynamic_index_in_dim(cache_keys, row_number, 0, keepdims=False)
        row_cache_values = lax.dynamic_index_in_dim(cached_value_rows, row_number, 0, keepdims=False)
        row_new_keys = lax.dynamic_index_in_dim(decode_keys, row_number, 1, keepdims=False)
        row_new_values = lax.dynamic_index_in_dim(decode_value_rows, row_number, 1, keepdims=False)
        row_keys = jnp.concatenate([row_cache_keys, slot_key_rows.transpose(1, 0, 2), row_new_keys.transpose(1, 0, 2)], axis=1)
        row_values = jnp.concatenate([row_cache_values, slot_value_rows.transpose(1, 0, 2), row_new_values.transpose(1, 0, 2)], axis=1)
        length = lax.dynamic_index_in_dim(cache_lengths, row_number, 0, keepdims=False)
        usable = jnp.concatenate([
            jnp.broadcast_to(cache_index[None, :] < length, (DECODE_STEPS, CACHE_SLOTS)),
            jnp.zeros((DECODE_STEPS, STRETCH_LENGTH), jnp.int32) == 0,
            step_index[None, :] <= step_index[:, None]], axis=1)
        scores = jnp.einsum("tsgd,skd->tsgk", row_query_matrix.astype(jnp.float32), row_keys.astype(jnp.float32)) * scaling
        scores = jnp.where(usable[:, None, None, :], scores, masked_score)
        row_max = jnp.max(scores, axis=-1, keepdims=True)
        weights = jnp.where(usable[:, None, None, :], jnp.exp(scores - row_max), 0.0)
        mixed = jnp.einsum("tsgk,skd->tsgd", weights, row_values.astype(jnp.float32), precision=lax.Precision.HIGHEST)
        return mixed / jnp.sum(weights, axis=-1)[..., None]

    decode_result = lax.map(decode_row, jnp.arange(DECODE_ROWS, dtype=jnp.int32))
    decode_output = decode_result.transpose(1, 0, 2, 3, 4).reshape(DECODE_STEPS, DECODE_ROWS, KEY_VALUE_HEADS, QUERY_GROUP * HEAD_SIZE).astype(jnp.bfloat16)
    return prefill_out, decode_output
```

```python
import functools

import jax
import jax.numpy as jnp
from jax import lax
from jax.experimental import pallas as pl
from jax.experimental.pallas import tpu as pltpu
from jax.sharding import PartitionSpec as P

HEAD = 128
GROUP = 8
BLOCK = 512
ROWS = 256
CACHE = 2048
NEG = -1e30
SCALE = HEAD**-0.5 * 1.4426950408889634
BF = jnp.bfloat16
F32 = jnp.float32
NT = (((1,), (1,)), ((), ()))
MESH = pl.DeviceIdType.MESH

OWN, L, R, O, Z, ZL, ZR, ZO = range(8)
ORDER = [
    (0, OWN),
    (1, OWN),
    (0, L),
    (0, R),
    (0, O),
    (1, L),
    (1, R),
    (0, Z),
    (0, ZL),
    (0, ZR),
    (1, O),
    (0, ZO),
    (1, Z),
    (1, ZL),
    (1, ZR),
    (1, ZO),
]


def nt_dot(a, b):
    return lax.dot_general(a, b, NT, preferred_element_type=F32)


def dot(a, b):
    return jnp.dot(a, b, preferred_element_type=F32)


def split(p):
    hi = p.astype(BF)
    return hi, (p - hi.astype(F32)).astype(BF)


def kernel(
    blocks,
    offset_ref,
    slot_index_ref,
    lengths_ref,
    q_ref,
    pk_ref,
    pv_ref,
    sk_ref,
    sv_ref,
    dq_ref,
    dk_ref,
    dv_ref,
    ck_hbm,
    cv_hbm,
    out_ref,
    dec_ref,
    ck,
    cv,
    qx,
    kbuf,
    vbuf,
    small,
    cand,
    scat,
    dqall,
    kst,
    vst,
    vslot,
    dres,
    dret,
    dec_o,
    dec_l,
    s_a,
    s_b,
    x_a,
    x_b,
    m_ref,
    l_ref,
    acc_ref,
    obuf,
    cbuf,
    ybuf,
    cache_sem,
    send_sem,
    recv_sem,
    small_send,
    small_recv,
    scat_send,
    scat_recv,
    dq_send,
    dq_recv,
    dret_send,
    dret_recv,
    core_send,
    core_recv,
    y_send,
    y_recv,
):
    c = lax.axis_index("ctx")
    t = lax.axis_index("tp")
    d = lax.axis_index("dec")
    zh, x = c // 4, c % 4
    y, co = d // 2, d % 2

    def ctx_at(dz, dx):
        return ((zh + dz) % 2) * 4 + (x + dx) % 4

    slots = {
        OWN: ctx_at(0, 0),
        L: ctx_at(0, 3),
        R: ctx_at(0, 1),
        O: ctx_at(0, 2),
        Z: ctx_at(1, 0),
        ZL: ctx_at(1, 3),
        ZR: ctx_at(1, 1),
        ZO: ctx_at(1, 2),
    }
    dev = {k: (slots[k], t, d) for k in (L, R, O, Z)}
    tp_peer = [(c, (t + i) % 4, d) for i in (1, 2, 3)]
    core_peer = (c, t, y * 2 + 1 - co)
    y_peer = [(c, t, ((y + i) % 4) * 2 + co) for i in (1, 2, 3)]

    def remote(src, dst, ss, rs, to):
        return pltpu.make_async_remote_copy(
            src_ref=src, dst_ref=dst, send_sem=ss, recv_sem=rs, device_id=to, device_id_type=MESH
        )

    def when(cond, f):
        if cond is True:
            f()
        else:
            pl.when(cond)(f)

    def exists(which):
        return True if blocks >= 8 else slots[which] < blocks

    cache_copies = []
    for r in range(4):
        for i, (hbm, vmem) in enumerate(((ck_hbm, ck), (cv_hbm, cv))):
            cp = pltpu.make_async_copy(hbm.at[r], vmem.at[r], cache_sem.at[r, i])
            cp.start()
            cache_copies.append(cp)

    row_id = lax.broadcasted_iota(jnp.int32, (BLOCK, HEAD), 0)
    lane_id = lax.broadcasted_iota(jnp.int32, (BLOCK, HEAD), 1)

    def fill(i, carry):
        limit = offset_ref[0] - (i * 8 + d) * BLOCK
        bias = jnp.where((lane_id == 0) & (row_id >= limit), NEG, 0.0).astype(BF)
        kbuf[0, i, :, HEAD:] = bias
        kbuf[1, i, :, HEAD:] = bias
        return carry

    lax.fori_loop(0, blocks, fill, 0)

    barrier = pltpu.get_barrier_semaphore()
    peers = [dev[L], dev[R], dev[O], dev[Z], *tp_peer, core_peer, *y_peer]
    for p in peers:
        pl.semaphore_signal(barrier, inc=1, device_id=p, device_id_type=MESH)

    me = slots[OWN]
    for h in range(2):
        kbuf[h, me, :, :HEAD] = pk_ref[:, h * HEAD : (h + 1) * HEAD]
        vbuf[h, me] = pv_ref[:, h * HEAD : (h + 1) * HEAD].T

    my_head = 0
    for h in range(8):
        my_head = my_head + jnp.where(slot_index_ref[h] == d, h, 0)
    odd = my_head % 2 == 1
    for i, ref in enumerate((sk_ref, sv_ref)):
        chosen = jnp.where(odd, ref[:, HEAD:], ref[:, :HEAD])
        for q in range(4):
            cand[q, i] = chosen[q * 64 : (q + 1) * 64]
        mine = pl.ds(pl.multiple_of(d * 32, 32), 32)
        for h in range(2):
            small[me, (2 * i + h) * 32 : (2 * i + h + 1) * 32, :] = ref[mine, h * HEAD : (h + 1) * HEAD]
    scat[t] = cand[t]
    dqall[t] = dq_ref[...]

    pl.semaphore_wait(barrier, len(peers))

    def copy_k(h, which, to, n):
        s = slots[which]
        ref = kbuf.at[h, s, :, pl.ds(0, HEAD)]
        return remote(ref, ref, send_sem.at[h, n], recv_sem.at[h, s, 0], dev[to])

    def copy_v(h, which, to, n):
        s = slots[which]
        ref = vbuf.at[h, s]
        return remote(ref, ref, send_sem.at[h, n], recv_sem.at[h, s, 1], dev[to])

    own_sends = [(OWN, 0, Z, 0), (OWN, 0, L, 1), (OWN, 0, R, 2), (OWN, 1, Z, 3), (OWN, 1, L, 4), (OWN, 1, R, 5)]
    z_sends = [(Z, 0, L, 6), (Z, 0, R, 7), (Z, 1, L, 8), (Z, 1, R, 9)]
    forwards = {
        L: [(L, 0, R, 10)],
        R: [(R, 1, L, 11)],
        ZL: [(ZL, 0, R, 12)],
        ZR: [(ZR, 1, L, 13)],
        Z: z_sends,
    }

    def make(h, s):
        return (copy_v if s[1] else copy_k)(h, s[0], s[2], s[3])

    def start_all(h, sends):
        for s in sends:
            make(h, s).start()

    def arrive(h, which):
        def go():
            copy_k(h, which, L, 0).wait_recv()
            copy_v(h, which, L, 0).wait_recv()
            start_all(h, forwards.get(which, []))

        when(exists(which), go)

    for h in range(2):
        when(exists(OWN), functools.partial(start_all, h, own_sends))
        if h == 0:
            scat_copies = []
            dq_copies = []
            for i in range(3):
                q = (t + 1 + i) % 4
                cp = remote(cand.at[q], scat.at[t], scat_send.at[i], scat_recv.at[t], tp_peer[i])
                cp.start()
                scat_copies.append(cp)
                cp = remote(dqall.at[t], dqall.at[t], dq_send.at[i], dq_recv.at[t], tp_peer[i])
                cp.start()
                dq_copies.append(cp)

    one_lane = (lax.broadcasted_iota(jnp.int32, (ROWS, HEAD), 1) == 0).astype(F32).astype(BF)
    for j in range(16):
        qx[j, :, :HEAD] = q_ref[:, j * HEAD : (j + 1) * HEAD]
        qx[j, :, HEAD:] = one_lane
    m_ref[...] = jnp.full(m_ref.shape, NEG, F32)
    l_ref[...] = jnp.zeros(l_ref.shape, F32)
    acc_ref[...] = jnp.zeros(acc_ref.shape, F32)

    def score(h, slot, g, s_ref, x_ref):
        keys = kbuf[h, slot]
        for u in range(2):
            s = nt_dot(keys, qx[h * 8 + g * 2 + u])
            s_ref[u] = s
            x_ref[u] = jnp.max(s, axis=0, keepdims=True) * SCALE

    def update(j, s, top, vt):
        before = m_ref[j]
        now = jnp.maximum(before, top)
        p = jnp.exp2(s * SCALE - now)
        fade = jnp.exp2(before - now)
        l_ref[j] = l_ref[j] * fade + jnp.sum(p, axis=0, keepdims=True)
        m_ref[j] = now
        hi, lo = split(p)
        acc_ref[j] = acc_ref[j] * fade + (dot(vt, hi) + dot(vt, lo))

    def absorb(h, slot, g, s_ref, x_ref):
        for u in range(2):
            update(h * 8 + g * 2 + u, s_ref[u], x_ref[u], vbuf[h, slot])

    def flash_block(h, slot):
        score(h, slot, 0, s_a, x_a)

        def body(i, carry):
            g = 2 * i
            score(h, slot, g + 1, s_b, x_b)
            absorb(h, slot, g, s_a, x_a)
            score(h, slot, jnp.minimum(g + 2, 3), s_a, x_a)
            absorb(h, slot, g + 1, s_b, x_b)
            return carry

        lax.fori_loop(0, 2, body, 0)

    def small_copy(which, to, n):
        ref = small.at[slots[which]]
        return remote(ref, ref, small_send.at[n], small_recv.at[slots[which]], dev[to])

    def pick_slot_share():
        for cp in dq_copies + scat_copies:
            cp.wait_send()
        for i in range(3):
            src = (t + 3 - i) % 4
            remote(cand.at[0], scat.at[src], scat_send.at[i], scat_recv.at[src], tp_peer[i]).wait_recv()
        source = my_head // 2
        for i in range(2):
            share = scat[0, i]
            for q in range(1, 4):
                share = jnp.where(source == q, scat[q, i], share)
            small[me, 128 + 64 * i : 192 + 64 * i, :] = share
        for n, to in enumerate((Z, L, R, O)):
            small_copy(OWN, to, n).start()

    def pass_small():
        small_copy(Z, L, 0).wait_recv()
        for n, to in enumerate((L, R, O)):
            small_copy(Z, to, 4 + n).start()

    def take_small():
        for which in (L, R, O, ZL, ZR, ZO):
            small_copy(which, L, 0).wait_recv()
        for h in range(2):
            kst[h] = small[:, h * 32 : (h + 1) * 32, :].reshape(ROWS, HEAD)
            vst[h] = small[:, 64 + h * 32 : 96 + h * 32, :].reshape(ROWS, HEAD).T
        vslot[...] = small[:, 192:256, :].reshape(BLOCK, HEAD).T

    def stretch_part():
        kk = lax.broadcasted_iota(jnp.int32, (ROWS, ROWS), 0)
        key_row = (kk // 32) * ROWS + d * 32 + kk % 32
        query_row = c * ROWS + lax.broadcasted_iota(jnp.int32, (ROWS, ROWS), 1)
        usable = key_row <= query_row

        def body(i, carry):
            h = i // 4
            for u in range(2):
                j = 2 * i + u
                s = jnp.where(usable, nt_dot(kst[h], qx[j, :, :HEAD]), NEG)
                update(j, s, jnp.max(s, axis=0, keepdims=True) * SCALE, vst[h])
            return carry

        lax.fori_loop(0, 8, body, 0)

    def decode_cache():
        for cp in cache_copies:
            cp.wait()
        step_row = lax.broadcasted_iota(jnp.int32, (16, 1), 0) >= 8
        for r in range(4):
            q = dq_ref[r * 16 : (r + 1) * 16, :]
            qf = q.astype(F32)
            s = nt_dot(q, ck[r]) * SCALE
            s = jnp.where(lax.broadcasted_iota(jnp.int32, (16, CACHE), 1) < lengths_ref[r], s, NEG)
            new = []
            for u in range(2):
                sn = jnp.sum(qf * dk_ref[u * 4 + r : u * 4 + r + 1, :].astype(F32), axis=1, keepdims=True) * SCALE
                new.append(jnp.where(step_row, sn, NEG) if u else sn)
            top = jnp.maximum(jnp.max(s, axis=1, keepdims=True), jnp.maximum(new[0], new[1]))
            p = jnp.exp2(s - top)
            pn = [jnp.exp2(sn - top) for sn in new]
            total = jnp.sum(p, axis=1, keepdims=True) + pn[0] + pn[1]
            hi, lo = split(p)
            mixed = dot(jnp.concatenate([hi, lo], axis=0), cv[r])
            mixed = mixed[:16] + mixed[16:]
            for u in range(2):
                mixed = mixed + pn[u] * dv_ref[u * 4 + r : u * 4 + r + 1, :].astype(F32)
            dec_o[r * 16 : (r + 1) * 16, :] = mixed / total
            dec_l[r * 16 : (r + 1) * 16, :] = jnp.broadcast_to(top + jnp.log2(total), (16, HEAD))

    dret_copies = [
        remote(dres.at[(t + 1 + i) % 4], dret.at[t], dret_send.at[i], dret_recv.at[t], tp_peer[i]) for i in range(3)
    ]

    def decode_stretch():
        for i in range(3):
            src = (t + 3 - i) % 4
            remote(dqall.at[src], dqall.at[src], dq_send.at[i], dq_recv.at[src], tp_peer[i]).wait_recv()
        keys = small[:, 128:192, :].reshape(BLOCK, HEAD)
        s = nt_dot(keys, dqall[...].reshape(4 * 64, HEAD)) * SCALE
        top = jnp.max(s, axis=0, keepdims=True)
        p = jnp.exp2(s - top)
        total = jnp.sum(p, axis=0, keepdims=True)
        hi, lo = split(p)
        o = ((dot(vslot[...], hi) + dot(vslot[...], lo)) / total).T
        lse = jnp.broadcast_to(top + jnp.log2(total), (HEAD, 256)).T
        for q in range(4):
            dres[q, 0] = o[q * 64 : (q + 1) * 64]
            dres[q, 1] = lse[q * 64 : (q + 1) * 64]
        dret[t] = dres[t]
        for cp in dret_copies:
            cp.start()

    def decode_finish():
        for i in range(3):
            src = (t + 3 - i) % 4
            remote(dres.at[0], dret.at[src], dret_send.at[i], dret_recv.at[src], tp_peer[i]).wait_recv()
        top = dec_l[...]
        for q in range(4):
            top = jnp.maximum(top, dret[q, 1])
        w = jnp.exp2(dec_l[...] - top)
        num, den = w * dec_o[...], w
        for q in range(4):
            w = jnp.exp2(dret[q, 1] - top)
            num, den = num + w * dret[q, 0], den + w
        dec_ref[...] = (num / den).astype(BF)

    def core_copy(h):
        return remote(obuf.at[h, 1 - co], cbuf.at[h], core_send.at[h], core_recv.at[h], core_peer)

    def y_copy(h, i):
        return remote(
            obuf.at[h, co, (y + 1 + i) % 4], ybuf.at[h, y], y_send.at[h, i], y_recv.at[h, y], y_peer[i]
        )

    def finish_head(h):
        def body(g, carry):
            j = h * 8 + g
            o = (acc_ref[j] / l_ref[j]).T
            for k in range(8):
                obuf[h, k % 2, k // 2, g] = o[k * 32 : (k + 1) * 32]
            return carry

        lax.fori_loop(0, 8, body, 0)
        lse = [m_ref[h * 8 + g] + jnp.log2(l_ref[h * 8 + g]) for g in range(8)]
        lse = jnp.concatenate(lse + [jnp.zeros((120, ROWS), F32)], axis=0).T
        for k in range(8):
            obuf[h, k % 2, k // 2, 8] = lse[k * 32 : (k + 1) * 32]
        core_copy(h).start()

    def merge_cores(h):
        core_copy(h).wait_recv()

        def body(i, carry):
            a, b = obuf[h, co, i, 8], cbuf[h, i, 8]
            top = jnp.maximum(a, b)
            wa, wb = jnp.exp2(a - top), jnp.exp2(b - top)
            both = wa + wb
            obuf[h, co, i, 8] = top + jnp.log2(both)
            wa, wb = wa / both, wb / both
            for g in range(8):
                obuf[h, co, i, g] = obuf[h, co, i, g] * wa[:, g : g + 1] + cbuf[h, i, g] * wb[:, g : g + 1]
            return carry

        lax.fori_loop(0, 4, body, 0)
        for i in range(3):
            y_copy(h, i).start()

    def merge_y(h):
        for i in range(3):
            src = (y + 3 - i) % 4
            remote(
                obuf.at[h, co, 0], ybuf.at[h, src], y_send.at[h, i], y_recv.at[h, src], y_peer[i]
            ).wait_recv()
        ybuf[h, y] = obuf[h, co, y]
        parts = [ybuf[h, i, 8] for i in range(4)]
        top = functools.reduce(jnp.maximum, parts)
        w = [jnp.exp2(p - top) for p in parts]
        inv = 1.0 / (w[0] + w[1] + w[2] + w[3])
        w = [a * inv for a in w]
        for g in range(8):
            o = ybuf[h, 0, g] * w[0][:, g : g + 1]
            for i in range(1, 4):
                o = o + ybuf[h, i, g] * w[i][:, g : g + 1]
            out_ref[:, (h * 8 + g) * HEAD : (h * 8 + g + 1) * HEAD] = o.astype(BF)

    ahead = {k: [] for k in range(17)}
    ahead[1] += [pick_slot_share]
    ahead[2] += [decode_cache, lambda: arrive(0, L)]
    ahead[3] += [lambda: arrive(0, R), pass_small]
    ahead[4] += [lambda: arrive(0, O), lambda: arrive(0, Z)]
    ahead[5] += [lambda: arrive(1, L)]
    ahead[6] += [lambda: arrive(1, R)]
    ahead[8] += [lambda: arrive(0, ZL), lambda: arrive(0, ZR)]
    ahead[10] += [lambda: arrive(1, O), lambda: arrive(1, Z)]
    ahead[11] += [take_small, stretch_part, decode_stretch, lambda: arrive(0, ZO)]
    ahead[12] += [lambda: finish_head(0)]
    ahead[13] += [lambda: merge_cores(0), lambda: arrive(1, ZL)]
    ahead[14] += [lambda: arrive(1, ZR), decode_finish]
    ahead[15] += [lambda: arrive(1, ZO)]

    def step(n, carry):
        h = 0
        slot = 0
        for k, (hk, which) in enumerate(ORDER):
            if hk:
                h = h + jnp.where(n == k, 1, 0)
            slot = slot + jnp.where(n == k, slots[which], 0)
            if ahead[k]:

                def go(k=k):
                    for f in ahead[k]:
                        f()

                pl.when(n == k)(go)
        when(True if blocks >= 8 else slot < blocks, lambda: flash_block(h, slot))
        return carry

    lax.fori_loop(0, 16, step, 0)
    finish_head(1)
    merge_cores(1)
    merge_y(0)
    merge_y(1)

    def own_done():
        for h in range(2):
            for s in own_sends:
                make(h, s).wait_send()

    when(exists(OWN), own_done)
    for which, sends in forwards.items():

        def fwd_done(sends=sends):
            for h in range(2):
                for s in sends:
                    make(h, s).wait_send()

        when(exists(which), fwd_done)
    for n, to in enumerate((Z, L, R, O)):
        small_copy(OWN, to, n).wait_send()
    for n, to in enumerate((L, R, O)):
        small_copy(Z, to, 4 + n).wait_send()
    for cp in dret_copies:
        cp.wait_send()
    for h in range(2):
        core_copy(h).wait_send()
        for i in range(3):
            y_copy(h, i).wait_send()


def fused(blocks, args):
    vmem = pl.BlockSpec(memory_space=pltpu.VMEM)
    smem = pl.BlockSpec(memory_space=pltpu.SMEM)
    anym = pl.BlockSpec(memory_space=pl.ANY)
    dma = pltpu.SemaphoreType.DMA
    return pl.pallas_call(
        functools.partial(kernel, blocks),
        out_shape=(
            jax.ShapeDtypeStruct((32, 2048), BF),
            jax.ShapeDtypeStruct((64, HEAD), BF),
        ),
        in_specs=[smem] * 3 + [vmem] * 8 + [anym] * 2,
        out_specs=(vmem, vmem),
        scratch_shapes=[
            pltpu.VMEM((4, CACHE, HEAD), BF),
            pltpu.VMEM((4, CACHE, HEAD), BF),
            pltpu.VMEM((16, ROWS, 2 * HEAD), BF),
            pltpu.VMEM((2, 8, BLOCK, 2 * HEAD), BF),
            pltpu.VMEM((2, 8, HEAD, BLOCK), BF),
            pltpu.VMEM((8, 256, HEAD), BF),
            pltpu.VMEM((4, 2, 64, HEAD), BF),
            pltpu.VMEM((4, 2, 64, HEAD), BF),
            pltpu.VMEM((4, 64, HEAD), BF),
            pltpu.VMEM((2, ROWS, HEAD), BF),
            pltpu.VMEM((2, HEAD, ROWS), BF),
            pltpu.VMEM((HEAD, BLOCK), BF),
            pltpu.VMEM((4, 2, 64, HEAD), F32),
            pltpu.VMEM((4, 2, 64, HEAD), F32),
            pltpu.VMEM((64, HEAD), F32),
            pltpu.VMEM((64, HEAD), F32),
            pltpu.VMEM((2, BLOCK, ROWS), F32),
            pltpu.VMEM((2, BLOCK, ROWS), F32),
            pltpu.VMEM((2, 1, ROWS), F32),
            pltpu.VMEM((2, 1, ROWS), F32),
            pltpu.VMEM((16, 1, ROWS), F32),
            pltpu.VMEM((16, 1, ROWS), F32),
            pltpu.VMEM((16, HEAD, ROWS), F32),
            pltpu.VMEM((2, 2, 4, 9, 32, HEAD), F32),
            pltpu.VMEM((2, 4, 9, 32, HEAD), F32),
            pltpu.VMEM((2, 4, 9, 32, HEAD), F32),
            dma((4, 2)),
            dma((2, 14)),
            dma((2, 8, 2)),
            dma((7,)),
            dma((8,)),
            dma((3,)),
            dma((4,)),
            dma((3,)),
            dma((4,)),
            dma((3,)),
            dma((4,)),
            dma((2,)),
            dma((2,)),
            dma((2, 3)),
            dma((2, 4)),
        ],
        compiler_params=pltpu.CompilerParams(
            collective_id=blocks, has_side_effects=True, vmem_limit_bytes=56 << 20
        ),
        name=f"attention_{blocks}",
    )(*args)


def shards(
    stretch_query_rows,
    stretch_key_rows,
    stretch_value_rows,
    prefix_key_rows,
    prefix_value_rows,
    offset,
    decode_query_rows,
    decode_keys,
    decode_value_rows,
    cache_keys,
    cached_value_rows,
    cache_lengths,
    head_slot_index,
):
    dq = decode_query_rows.reshape(2, 4, GROUP, HEAD).transpose(1, 0, 2, 3).reshape(64, HEAD)
    args = (
        offset,
        head_slot_index,
        cache_lengths,
        stretch_query_rows,
        prefix_key_rows,
        prefix_value_rows,
        stretch_key_rows,
        stretch_value_rows,
        dq,
        decode_keys.reshape(8, HEAD),
        decode_value_rows.reshape(8, HEAD),
        cache_keys.reshape(4, CACHE, HEAD),
        cached_value_rows.reshape(4, CACHE, HEAD),
    )
    prefill_out, dec = fused(8, args)
    decode_output = dec.reshape(4, 2, GROUP, HEAD).transpose(1, 0, 2, 3).reshape(2, 4, 1, GROUP * HEAD)
    return prefill_out, decode_output


def solution(mesh):
    placed = (
        P("ctx", "tp"),
        P("ctx", "tp"),
        P("ctx", "tp"),
        P(("ctx", "dec"), "tp"),
        P(("ctx", "dec"), "tp"),
        P(),
        P(None, ("ctx", "tp"), "dec", None),
        P(None, ("ctx", "tp"), "dec", None),
        P(None, ("ctx", "tp"), "dec", None),
        P(("ctx", "tp"), "dec", None, None),
        P(("ctx", "tp"), "dec", None, None),
        P(("ctx", "tp")),
        P(),
    )
    return jax.shard_map(
        shards,
        mesh=mesh,
        in_specs=placed,
        out_specs=(P(("ctx", "dec"), "tp"), P(None, ("ctx", "tp"), "dec", None)),
        check_vma=False,
    )
```

```python
import functools

import jax
import jax.numpy as jnp
from jax import lax
from jax.experimental import pallas as pl
from jax.experimental.pallas import tpu as pltpu
from jax.sharding import PartitionSpec as P

HEAD = 128
GROUP = 8
BLOCK = 512
ROWS = 256
CACHE = 2048
NEG = -1e30
SCALE = HEAD**-0.5 * 1.4426950408889634
BF = jnp.bfloat16
F32 = jnp.float32
NT = (((1,), (1,)), ((), ()))
MESH = pl.DeviceIdType.MESH

OWN, L, R, O, Z, ZL, ZR, ZO = range(8)
ORDER = [
    (0, OWN),
    (1, OWN),
    (0, L),
    (0, R),
    (1, L),
    (1, R),
    (0, Z),
    (0, O),
    (1, O),
    (1, Z),
    (0, ZL),
    (0, ZR),
    (0, ZO),
    (1, ZL),
    (1, ZR),
    (1, ZO),
]


def nt_dot(a, b):
    return lax.dot_general(a, b, NT, preferred_element_type=F32)


def dot(a, b):
    return jnp.dot(a, b, preferred_element_type=F32)


def split(p):
    hi = p.astype(BF)
    return hi, (p - hi.astype(F32)).astype(BF)


def kernel(
    blocks,
    offset_ref,
    slot_index_ref,
    lengths_ref,
    q_ref,
    pk_ref,
    pv_ref,
    sk_ref,
    sv_ref,
    dq_ref,
    dk_ref,
    dv_ref,
    ck_hbm,
    cv_hbm,
    out_ref,
    dec_ref,
    ck,
    cv,
    qx,
    kbuf,
    vbuf,
    share,
    slot_rows,
    cand,
    scat,
    dq_rows,
    dqall,
    kst,
    vst,
    vslot,
    dres,
    dret,
    dec_o,
    dec_l,
    s_a,
    s_b,
    x_a,
    x_b,
    m_ref,
    l_ref,
    acc_ref,
    obuf,
    cbuf,
    ybuf,
    cache_sem,
    send_sem,
    recv_sem,
    share_send,
    share_recv,
    slot_send,
    slot_recv,
    scat_send,
    scat_recv,
    dq_send,
    dq_recv,
    dret_send,
    dret_recv,
    core_send,
    core_recv,
    y_send,
    y_recv,
):
    c = lax.axis_index("ctx")
    t = lax.axis_index("tp")
    d = lax.axis_index("dec")
    zh, x = c // 4, c % 4
    y, co = d // 2, d % 2

    def ctx_at(dz, dx):
        return ((zh + dz) % 2) * 4 + (x + dx) % 4

    slots = {
        OWN: ctx_at(0, 0),
        L: ctx_at(0, 3),
        R: ctx_at(0, 1),
        O: ctx_at(0, 2),
        Z: ctx_at(1, 0),
        ZL: ctx_at(1, 3),
        ZR: ctx_at(1, 1),
        ZO: ctx_at(1, 2),
    }
    dev = {k: (slots[k], t, d) for k in (L, R, O, Z)}
    tp_peer = [(c, (t + i) % 4, d) for i in (1, 2, 3)]
    core_peer = (c, t, y * 2 + 1 - co)
    y_peer = [(c, t, ((y + i) % 4) * 2 + co) for i in (1, 2, 3)]

    def remote(src, dst, ss, rs, to):
        return pltpu.make_async_remote_copy(
            src_ref=src, dst_ref=dst, send_sem=ss, recv_sem=rs, device_id=to, device_id_type=MESH
        )

    def when(cond, f):
        if cond is True:
            f()
        else:
            pl.when(cond)(f)

    def exists(which):
        return True if blocks >= 8 else slots[which] < blocks

    cache_copies = []
    for r in range(4):
        for i, (hbm, vmem) in enumerate(((ck_hbm, ck), (cv_hbm, cv))):
            cp = pltpu.make_async_copy(hbm.at[r], vmem.at[r], cache_sem.at[r, i])
            cp.start()
            cache_copies.append(cp)

    row_id = lax.broadcasted_iota(jnp.int32, (BLOCK, HEAD), 0)
    lane_id = lax.broadcasted_iota(jnp.int32, (BLOCK, HEAD), 1)

    def fill(i, carry):
        limit = offset_ref[0] - (i * 8 + d) * BLOCK
        bias = jnp.where((lane_id == 0) & (row_id >= limit), NEG, 0.0).astype(BF)
        kbuf[0, i, :, HEAD:] = bias
        kbuf[1, i, :, HEAD:] = bias
        return carry

    lax.fori_loop(0, blocks, fill, 0)

    barrier = pltpu.get_barrier_semaphore()
    peers = [dev[L], dev[R], dev[O], dev[Z], *tp_peer, core_peer, *y_peer]
    for p in peers:
        pl.semaphore_signal(barrier, inc=1, device_id=p, device_id_type=MESH)

    me = slots[OWN]
    for h in range(2):
        kbuf[h, me, :, :HEAD] = pk_ref[:, h * HEAD : (h + 1) * HEAD]
        vbuf[h, me] = pv_ref[:, h * HEAD : (h + 1) * HEAD].T

    my_head = 0
    for h in range(8):
        my_head = my_head + jnp.where(slot_index_ref[h] == d, h, 0)
    odd = my_head % 2 == 1
    for i, ref in enumerate((sk_ref, sv_ref)):
        chosen = jnp.where(odd, ref[:, HEAD:], ref[:, :HEAD])
        for q in range(4):
            cand[q, i] = chosen[q * 64 : (q + 1) * 64]
        mine = pl.ds(pl.multiple_of(d * 32, 32), 32)
        for h in range(2):
            share[me, (2 * i + h) * 32 : (2 * i + h + 1) * 32, :] = ref[mine, h * HEAD : (h + 1) * HEAD]
    scat[t] = cand[t]
    for u in range(2):
        wide = dq_ref[u].astype(F32)
        for g in range(GROUP):
            at = (u * GROUP + g) * 4
            dq_rows[at : at + 4, :] = wide[:, g * HEAD : (g + 1) * HEAD]
    dqall[t] = dq_rows[...].astype(BF)

    pl.semaphore_wait(barrier, len(peers))

    def copy_k(h, which, to, n):
        s = slots[which]
        ref = kbuf.at[h, s, :, pl.ds(0, HEAD)]
        return remote(ref, ref, send_sem.at[h, n], recv_sem.at[h, s, 0], dev[to])

    def copy_v(h, which, to, n):
        s = slots[which]
        ref = vbuf.at[h, s]
        return remote(ref, ref, send_sem.at[h, n], recv_sem.at[h, s, 1], dev[to])

    own_sends = [(OWN, 0, Z, 0), (OWN, 0, L, 1), (OWN, 0, R, 2), (OWN, 1, Z, 3), (OWN, 1, L, 4), (OWN, 1, R, 5)]
    z_sends = [(Z, 0, L, 6), (Z, 0, R, 7), (Z, 1, L, 8), (Z, 1, R, 9)]
    forwards = {
        L: [(L, 0, R, 10)],
        R: [(R, 1, L, 11)],
        ZL: [(ZL, 0, R, 12)],
        ZR: [(ZR, 1, L, 13)],
        Z: z_sends,
    }

    def make(h, s):
        return (copy_v if s[1] else copy_k)(h, s[0], s[2], s[3])

    def start_all(h, sends):
        for s in sends:
            make(h, s).start()

    def arrive_one(h, which, kv):
        def go():
            (copy_v if kv else copy_k)(h, which, L, 0).wait_recv()
            start_all(h, [f for f in forwards.get(which, []) if f[1] == kv])

        when(exists(which), go)

    def arrive(h, which):
        arrive_one(h, which, 0)
        arrive_one(h, which, 1)

    def share_copy(buf, ss, rs, which, to, n):
        ref = buf.at[slots[which]]
        return remote(ref, ref, ss.at[n], rs.at[slots[which]], dev[to])

    stretch_share = functools.partial(share_copy, share, share_send, share_recv)
    slot_share = functools.partial(share_copy, slot_rows, slot_send, slot_recv)

    def send_share(copy):
        for n, to in enumerate((Z, L, R, O)):
            copy(OWN, to, n).start()

    def pass_share(copy):
        copy(Z, L, 0).wait_recv()
        for n, to in enumerate((L, R, O)):
            copy(Z, to, 4 + n).start()

    def take_share(copy):
        for which in (L, R, O, ZL, ZR, ZO):
            copy(which, L, 0).wait_recv()

    def share_done(copy):
        for n, to in enumerate((Z, L, R, O)):
            copy(OWN, to, n).wait_send()
        for n, to in enumerate((L, R, O)):
            copy(Z, to, 4 + n).wait_send()

    scat_copies = []
    dq_copies = []
    for i in range(3):
        q = (t + 1 + i) % 4
        cp = remote(cand.at[q], scat.at[t], scat_send.at[i], scat_recv.at[t], tp_peer[i])
        cp.start()
        scat_copies.append(cp)
        cp = remote(dqall.at[t], dqall.at[t], dq_send.at[i], dq_recv.at[t], tp_peer[i])
        cp.start()
        dq_copies.append(cp)

    def start_own():
        start_all(0, own_sends)
        start_all(1, own_sends)

    send_share(stretch_share)
    when(exists(OWN), start_own)

    one_lane = (lax.broadcasted_iota(jnp.int32, (ROWS, HEAD), 1) == 0).astype(F32).astype(BF)
    for j in range(16):
        qx[j, :, :HEAD] = q_ref[:, j * HEAD : (j + 1) * HEAD]
        qx[j, :, HEAD:] = one_lane
    m_ref[...] = jnp.full(m_ref.shape, NEG, F32)
    l_ref[...] = jnp.zeros(l_ref.shape, F32)
    acc_ref[...] = jnp.zeros(acc_ref.shape, F32)

    def score(h, slot, g, s_ref, x_ref):
        keys = kbuf[h, slot]
        for u in range(2):
            s = nt_dot(keys, qx[h * 8 + g * 2 + u])
            s_ref[u] = s
            x_ref[u] = jnp.max(s, axis=0, keepdims=True) * SCALE

    def update(j, s, top, vt):
        before = m_ref[j]
        now = jnp.maximum(before, top)
        p = jnp.exp2(s * SCALE - now)
        fade = jnp.exp2(before - now)
        l_ref[j] = l_ref[j] * fade + jnp.sum(p, axis=0, keepdims=True)
        m_ref[j] = now
        hi, lo = split(p)
        acc_ref[j] = acc_ref[j] * fade + (dot(vt, hi) + dot(vt, lo))

    def absorb(h, slot, g, s_ref, x_ref):
        for u in range(2):
            update(h * 8 + g * 2 + u, s_ref[u], x_ref[u], vbuf[h, slot])

    def flash_block(h, slot):
        score(h, slot, 0, s_a, x_a)
        score(h, slot, 1, s_b, x_b)
        absorb(h, slot, 0, s_a, x_a)
        score(h, slot, 2, s_a, x_a)
        absorb(h, slot, 1, s_b, x_b)
        score(h, slot, 3, s_b, x_b)
        absorb(h, slot, 2, s_a, x_a)
        absorb(h, slot, 3, s_b, x_b)

    def pick_slot_share():
        for cp in dq_copies + scat_copies:
            cp.wait_send()
        for i in range(3):
            src = (t + 3 - i) % 4
            remote(cand.at[0], scat.at[src], scat_send.at[i], scat_recv.at[src], tp_peer[i]).wait_recv()
        source = my_head // 2
        for i in range(2):
            quarter = scat[0, i]
            for q in range(1, 4):
                quarter = jnp.where(source == q, scat[q, i], quarter)
            slot_rows[me, 64 * i : 64 * i + 64, :] = quarter
        send_share(slot_share)

    def stretch_part():
        take_share(stretch_share)
        for h in range(2):
            kst[h] = share[:, h * 32 : (h + 1) * 32, :].reshape(ROWS, HEAD)
            vst[h] = share[:, 64 + h * 32 : 96 + h * 32, :].reshape(ROWS, HEAD).T
        kk = lax.broadcasted_iota(jnp.int32, (ROWS, ROWS), 0)
        key_row = (kk // 32) * ROWS + d * 32 + kk % 32
        query_row = c * ROWS + lax.broadcasted_iota(jnp.int32, (ROWS, ROWS), 1)
        usable = key_row <= query_row

        def stretch_score(h, g, s_ref, x_ref):
            for u in range(2):
                s = jnp.where(usable, nt_dot(kst[h], qx[h * 8 + g * 2 + u, :, :HEAD]), NEG)
                s_ref[u, :ROWS] = s
                x_ref[u] = jnp.max(s, axis=0, keepdims=True) * SCALE

        def stretch_absorb(h, g, s_ref, x_ref):
            for u in range(2):
                update(h * 8 + g * 2 + u, s_ref[u, :ROWS], x_ref[u], vst[h])

        def body(h, carry):
            stretch_score(h, 0, s_a, x_a)
            stretch_score(h, 1, s_b, x_b)
            stretch_absorb(h, 0, s_a, x_a)
            stretch_score(h, 2, s_a, x_a)
            stretch_absorb(h, 1, s_b, x_b)
            stretch_score(h, 3, s_b, x_b)
            stretch_absorb(h, 2, s_a, x_a)
            stretch_absorb(h, 3, s_b, x_b)
            return carry

        lax.fori_loop(0, 2, body, 0)

    def decode_cache():
        for cp in cache_copies:
            cp.wait()
        step_row = lax.broadcasted_iota(jnp.int32, (16, 1), 0) >= 8
        for r in range(4):
            qf = dq_rows[pl.ds(r, 16, stride=4), :]
            s = nt_dot(qf.astype(BF), ck[r]) * SCALE
            s = jnp.where(lax.broadcasted_iota(jnp.int32, (16, CACHE), 1) < lengths_ref[r], s, NEG)
            new = []
            for u in range(2):
                sn = jnp.sum(qf * dk_ref[u].astype(F32)[r : r + 1, :], axis=1, keepdims=True) * SCALE
                new.append(jnp.where(step_row, sn, NEG) if u else sn)
            top = jnp.maximum(jnp.max(s, axis=1, keepdims=True), jnp.maximum(new[0], new[1]))
            p = jnp.exp2(s - top)
            pn = [jnp.exp2(sn - top) for sn in new]
            total = jnp.sum(p, axis=1, keepdims=True) + pn[0] + pn[1]
            hi, lo = split(p)
            mixed = dot(jnp.concatenate([hi, lo], axis=0), cv[r])
            mixed = mixed[:16] + mixed[16:]
            for u in range(2):
                mixed = mixed + pn[u] * dv_ref[u].astype(F32)[r : r + 1, :]
            dec_o[pl.ds(r, 16, stride=4), :] = mixed / total
            dec_l[pl.ds(r, 16, stride=4), :] = jnp.broadcast_to(top + jnp.log2(total), (16, HEAD))

    dret_copies = [
        remote(dres.at[(t + 1 + i) % 4], dret.at[t], dret_send.at[i], dret_recv.at[t], tp_peer[i]) for i in range(3)
    ]

    def decode_stretch():
        take_share(slot_share)
        vslot[...] = slot_rows[:, 64:128, :].reshape(BLOCK, HEAD).T
        for i in range(3):
            src = (t + 3 - i) % 4
            remote(dqall.at[src], dqall.at[src], dq_send.at[i], dq_recv.at[src], tp_peer[i]).wait_recv()
        keys = slot_rows[:, 0:64, :].reshape(BLOCK, HEAD)
        s = nt_dot(keys, dqall[...].reshape(4 * 64, HEAD)) * SCALE
        top = jnp.max(s, axis=0, keepdims=True)
        p = jnp.exp2(s - top)
        total = jnp.sum(p, axis=0, keepdims=True)
        hi, lo = split(p)
        o = ((dot(vslot[...], hi) + dot(vslot[...], lo)) / total).T
        lse = jnp.broadcast_to(top + jnp.log2(total), (HEAD, 256)).T
        for q in range(4):
            dres[q, 0] = o[q * 64 : (q + 1) * 64]
            dres[q, 1] = lse[q * 64 : (q + 1) * 64]
        dret[t] = dres[t]
        for cp in dret_copies:
            cp.start()

    def decode_finish():
        for i in range(3):
            src = (t + 3 - i) % 4
            remote(dres.at[0], dret.at[src], dret_send.at[i], dret_recv.at[src], tp_peer[i]).wait_recv()
        top = dec_l[...]
        for q in range(4):
            top = jnp.maximum(top, dret[q, 1])
        w = jnp.exp2(dec_l[...] - top)
        num, den = w * dec_o[...], w
        for q in range(4):
            w = jnp.exp2(dret[q, 1] - top)
            num, den = num + w * dret[q, 0], den + w
        res = num / den
        for u in range(2):
            for g in range(GROUP):
                at = (u * GROUP + g) * 4
                dec_ref[u, :, g * HEAD : (g + 1) * HEAD] = res[at : at + 4, :].astype(BF)

    def core_copy(h):
        return remote(obuf.at[h, 1 - co], cbuf.at[h], core_send.at[h], core_recv.at[h], core_peer)

    def y_copy(h, i):
        return remote(
            obuf.at[h, co, (y + 1 + i) % 4], ybuf.at[h, y], y_send.at[h, i], y_recv.at[h, y], y_peer[i]
        )

    def finish_head(h):
        def body(g, carry):
            j = h * 8 + g
            o = (acc_ref[j] / l_ref[j]).T
            for k in range(8):
                obuf[h, k % 2, k // 2, g] = o[k * 32 : (k + 1) * 32]
            return carry

        lax.fori_loop(0, 8, body, 0)
        lse = [m_ref[h * 8 + g] + jnp.log2(l_ref[h * 8 + g]) for g in range(8)]
        lse = jnp.concatenate(lse + [jnp.zeros((120, ROWS), F32)], axis=0).T
        for k in range(8):
            obuf[h, k % 2, k // 2, 8] = lse[k * 32 : (k + 1) * 32]
        core_copy(h).start()

    def merge_cores(h):
        core_copy(h).wait_recv()

        def body(i, carry):
            a, b = obuf[h, co, i, 8], cbuf[h, i, 8]
            top = jnp.maximum(a, b)
            wa, wb = jnp.exp2(a - top), jnp.exp2(b - top)
            both = wa + wb
            obuf[h, co, i, 8] = top + jnp.log2(both)
            wa, wb = wa / both, wb / both
            for g in range(8):
                obuf[h, co, i, g] = obuf[h, co, i, g] * wa[:, g : g + 1] + cbuf[h, i, g] * wb[:, g : g + 1]
            return carry

        lax.fori_loop(0, 4, body, 0)
        for i in range(3):
            y_copy(h, i).start()

    def merge_y(h):
        for i in range(3):
            src = (y + 3 - i) % 4
            remote(
                obuf.at[h, co, 0], ybuf.at[h, src], y_send.at[h, i], y_recv.at[h, src], y_peer[i]
            ).wait_recv()
        ybuf[h, y] = obuf[h, co, y]
        parts = [ybuf[h, i, 8] for i in range(4)]
        top = functools.reduce(jnp.maximum, parts)
        w = [jnp.exp2(p - top) for p in parts]
        inv = 1.0 / (w[0] + w[1] + w[2] + w[3])
        w = [a * inv for a in w]
        for g in range(8):
            o = ybuf[h, 0, g] * w[0][:, g : g + 1]
            for i in range(1, 4):
                o = o + ybuf[h, i, g] * w[i][:, g : g + 1]
            out_ref[:, (h * 8 + g) * HEAD : (h * 8 + g + 1) * HEAD] = o.astype(BF)

    ahead = {k: [] for k in range(16)}
    ahead[2] += [lambda: arrive(0, L), lambda: arrive(0, R)]
    ahead[4] += [decode_cache, lambda: arrive(1, L), lambda: arrive(1, R), lambda: arrive_one(0, Z, 0)]
    ahead[5] += [lambda: arrive_one(0, Z, 1)]
    ahead[6] += [pick_slot_share, lambda: pass_share(stretch_share)]
    ahead[7] += [lambda: arrive(0, O)]
    ahead[8] += [lambda: arrive_one(1, Z, 0), lambda: arrive(1, O)]
    ahead[9] += [lambda: arrive_one(1, Z, 1)]
    ahead[10] += [lambda: arrive(0, ZL), lambda: arrive(0, ZR)]
    ahead[11] += [lambda: pass_share(slot_share)]
    ahead[12] += [stretch_part, lambda: arrive(0, ZO)]
    ahead[13] += [lambda: arrive(1, ZL), lambda: arrive(1, ZR), lambda: finish_head(0)]
    ahead[14] += [lambda: merge_cores(0)]
    ahead[15] += [lambda: arrive(1, ZO)]

    def step(n, carry):
        h = 0
        slot = 0
        for k, (hk, which) in enumerate(ORDER):
            if hk:
                h = h + jnp.where(n == k, 1, 0)
            slot = slot + jnp.where(n == k, slots[which], 0)
            if ahead[k]:

                def go(k=k):
                    for f in ahead[k]:
                        f()

                pl.when(n == k)(go)
        when(True if blocks >= 8 else slot < blocks, lambda: flash_block(h, slot))
        return carry

    lax.fori_loop(0, 16, step, 0)
    finish_head(1)
    decode_stretch()
    merge_cores(1)
    merge_y(0)
    decode_finish()
    merge_y(1)

    def own_done():
        for h in range(2):
            for s in own_sends:
                make(h, s).wait_send()

    when(exists(OWN), own_done)
    for which, sends in forwards.items():

        def fwd_done(sends=sends):
            for h in range(2):
                for s in sends:
                    make(h, s).wait_send()

        when(exists(which), fwd_done)
    share_done(stretch_share)
    share_done(slot_share)
    for cp in dret_copies:
        cp.wait_send()
    for h in range(2):
        core_copy(h).wait_send()
        for i in range(3):
            y_copy(h, i).wait_send()


def fused(blocks, args):
    vmem = pl.BlockSpec(memory_space=pltpu.VMEM)
    smem = pl.BlockSpec(memory_space=pltpu.SMEM)
    anym = pl.BlockSpec(memory_space=pl.ANY)
    dma = pltpu.SemaphoreType.DMA
    return pl.pallas_call(
        functools.partial(kernel, blocks),
        out_shape=(
            jax.ShapeDtypeStruct((32, 2048), BF),
            jax.ShapeDtypeStruct((2, 4, GROUP * HEAD), BF),
        ),
        in_specs=[smem] * 3 + [vmem] * 8 + [anym] * 2,
        out_specs=(vmem, vmem),
        scratch_shapes=[
            pltpu.VMEM((4, CACHE, HEAD), BF),
            pltpu.VMEM((4, CACHE, HEAD), BF),
            pltpu.VMEM((16, ROWS, 2 * HEAD), BF),
            pltpu.VMEM((2, 8, BLOCK, 2 * HEAD), BF),
            pltpu.VMEM((2, 8, HEAD, BLOCK), BF),
            pltpu.VMEM((8, 128, HEAD), BF),
            pltpu.VMEM((8, 128, HEAD), BF),
            pltpu.VMEM((4, 2, 64, HEAD), BF),
            pltpu.VMEM((4, 2, 64, HEAD), BF),
            pltpu.VMEM((64, HEAD), F32),
            pltpu.VMEM((4, 64, HEAD), BF),
            pltpu.VMEM((2, ROWS, HEAD), BF),
            pltpu.VMEM((2, HEAD, ROWS), BF),
            pltpu.VMEM((HEAD, BLOCK), BF),
            pltpu.VMEM((4, 2, 64, HEAD), F32),
            pltpu.VMEM((4, 2, 64, HEAD), F32),
            pltpu.VMEM((64, HEAD), F32),
            pltpu.VMEM((64, HEAD), F32),
            pltpu.VMEM((2, BLOCK, ROWS), F32),
            pltpu.VMEM((2, BLOCK, ROWS), F32),
            pltpu.VMEM((2, 1, ROWS), F32),
            pltpu.VMEM((2, 1, ROWS), F32),
            pltpu.VMEM((16, 1, ROWS), F32),
            pltpu.VMEM((16, 1, ROWS), F32),
            pltpu.VMEM((16, HEAD, ROWS), F32),
            pltpu.VMEM((2, 2, 4, 9, 32, HEAD), F32),
            pltpu.VMEM((2, 4, 9, 32, HEAD), F32),
            pltpu.VMEM((2, 4, 9, 32, HEAD), F32),
            dma((4, 2)),
            dma((2, 14)),
            dma((2, 8, 2)),
            dma((7,)),
            dma((8,)),
            dma((7,)),
            dma((8,)),
            dma((3,)),
            dma((4,)),
            dma((3,)),
            dma((4,)),
            dma((3,)),
            dma((4,)),
            dma((2,)),
            dma((2,)),
            dma((2, 3)),
            dma((2, 4)),
        ],
        compiler_params=pltpu.CompilerParams(
            collective_id=blocks, has_side_effects=True, vmem_limit_bytes=56 << 20
        ),
        name=f"attention_{blocks}",
    )(*args)


def shards(
    stretch_query_rows,
    stretch_key_rows,
    stretch_value_rows,
    prefix_key_rows,
    prefix_value_rows,
    offset,
    decode_query_rows,
    decode_keys,
    decode_value_rows,
    cache_keys,
    cached_value_rows,
    cache_lengths,
    head_slot_index,
):
    args = (
        offset,
        head_slot_index,
        cache_lengths,
        stretch_query_rows,
        prefix_key_rows,
        prefix_value_rows,
        stretch_key_rows,
        stretch_value_rows,
        decode_query_rows.reshape(2, 4, GROUP * HEAD),
        decode_keys.reshape(2, 4, HEAD),
        decode_value_rows.reshape(2, 4, HEAD),
        cache_keys.reshape(4, CACHE, HEAD),
        cached_value_rows.reshape(4, CACHE, HEAD),
    )
    prefill_out, dec = fused(8, args)
    return prefill_out, dec.reshape(2, 4, 1, GROUP * HEAD)


def solution(mesh):
    placed = (
        P("ctx", "tp"),
        P("ctx", "tp"),
        P("ctx", "tp"),
        P(("ctx", "dec"), "tp"),
        P(("ctx", "dec"), "tp"),
        P(),
        P(None, ("ctx", "tp"), "dec", None),
        P(None, ("ctx", "tp"), "dec", None),
        P(None, ("ctx", "tp"), "dec", None),
        P(("ctx", "tp"), "dec", None, None),
        P(("ctx", "tp"), "dec", None, None),
        P(("ctx", "tp")),
        P(),
    )
    return jax.shard_map(
        shards,
        mesh=mesh,
        in_specs=placed,
        out_specs=(P(("ctx", "dec"), "tp"), P(None, ("ctx", "tp"), "dec", None)),
        check_vma=False,
    )
```

```python
import functools

import jax
import jax.numpy as jnp
from jax import lax
from jax.experimental import pallas as pl
from jax.experimental.pallas import tpu as pltpu
from jax.sharding import PartitionSpec as P

HEAD = 128
GROUP = 8
BLOCK = 512
ROWS = 256
CACHE = 2048
NEG = -1e30
SCALE = HEAD**-0.5 * 1.4426950408889634
BF = jnp.bfloat16
F32 = jnp.float32
NT = (((1,), (1,)), ((), ()))
MESH = pl.DeviceIdType.MESH

OWN, L, R, O, Z, ZL, ZR, ZO = range(8)
MINE, PAIR = range(2)
ORDER = [
    (1, OWN, MINE),
    (0, OWN, MINE),
    (1, L, MINE),
    (1, R, MINE),
    (1, OWN, PAIR),
    (1, L, PAIR),
    (1, R, PAIR),
    (1, O, MINE),
    (1, O, PAIR),
    (0, L, MINE),
    (0, R, MINE),
    (0, O, MINE),
    (0, Z, MINE),
    (0, ZL, MINE),
    (0, ZR, MINE),
    (0, ZO, MINE),
]


def nt_dot(a, b):
    return lax.dot_general(a, b, NT, preferred_element_type=F32)


def dot(a, b):
    return jnp.dot(a, b, preferred_element_type=F32)


def split(p):
    hi = p.astype(BF)
    return hi, (p - hi.astype(F32)).astype(BF)


def kernel(
    blocks,
    offset_ref,
    slot_index_ref,
    lengths_ref,
    q_ref,
    pk_ref,
    pv_ref,
    sk_ref,
    sv_ref,
    dq_ref,
    dk_ref,
    dv_ref,
    ck_hbm,
    cv_hbm,
    out_ref,
    dec_ref,
    ck,
    cv,
    qx,
    kbuf,
    vbuf,
    q_pair,
    q_all,
    share,
    slot_rows,
    cand,
    scat,
    dq_rows,
    dqall,
    kst,
    vst,
    vslot,
    dres,
    dret,
    dec_o,
    dec_l,
    s_a,
    s_b,
    x_a,
    x_b,
    m_ref,
    l_ref,
    acc_ref,
    obuf,
    cbuf,
    ybuf,
    zbuf,
    cache_sem,
    send_sem,
    recv_sem,
    share_send,
    share_recv,
    slot_send,
    slot_recv,
    scat_send,
    scat_recv,
    dq_send,
    dq_recv,
    dret_send,
    dret_recv,
    core_send,
    core_recv,
    y_send,
    y_recv,
    pair_sem,
    q_send,
    q_recv,
    back_sem,
):
    c = lax.axis_index("ctx")
    t = lax.axis_index("tp")
    d = lax.axis_index("dec")
    zh, x = c // 4, c % 4
    y, co = d // 2, d % 2

    def ctx_at(dz, dx):
        return ((zh + dz) % 2) * 4 + (x + dx) % 4

    slots = {
        OWN: ctx_at(0, 0),
        L: ctx_at(0, 3),
        R: ctx_at(0, 1),
        O: ctx_at(0, 2),
        Z: ctx_at(1, 0),
        ZL: ctx_at(1, 3),
        ZR: ctx_at(1, 1),
        ZO: ctx_at(1, 2),
    }
    dev = {k: (slots[k], t, d) for k in (L, R, O, Z)}
    tp_peer = [(c, (t + i) % 4, d) for i in (1, 2, 3)]
    core_peer = (c, t, y * 2 + 1 - co)
    y_peer = [(c, t, ((y + i) % 4) * 2 + co) for i in (1, 2, 3)]
    dec_peer = [(c, t, (d + i) % 8) for i in range(1, 8)]

    def remote(src, dst, ss, rs, to):
        return pltpu.make_async_remote_copy(
            src_ref=src, dst_ref=dst, send_sem=ss, recv_sem=rs, device_id=to, device_id_type=MESH
        )

    def when(cond, f):
        if cond is True:
            f()
        else:
            pl.when(cond)(f)

    def exists(which):
        return True if blocks >= 8 else slots[which] < blocks

    cache_copies = []
    for r in range(4):
        for i, (hbm, vmem) in enumerate(((ck_hbm, ck), (cv_hbm, cv))):
            cp = pltpu.make_async_copy(hbm.at[r], vmem.at[r], cache_sem.at[r, i])
            cp.start()
            cache_copies.append(cp)

    row_id = lax.broadcasted_iota(jnp.int32, (BLOCK, HEAD), 0)
    lane_id = lax.broadcasted_iota(jnp.int32, (BLOCK, HEAD), 1)

    def fill(i, carry):
        limit = offset_ref[0] - (i * 8 + d) * BLOCK
        bias = jnp.where((lane_id == 0) & (row_id >= limit), NEG, 0.0).astype(BF)
        kbuf[0, i, :, HEAD:] = bias
        kbuf[1, i, :, HEAD:] = bias
        return carry

    lax.fori_loop(0, blocks, fill, 0)

    barrier = pltpu.get_barrier_semaphore()
    peers = [dev[L], dev[R], dev[O], dev[Z], *tp_peer, *dec_peer]
    for p in peers:
        pl.semaphore_signal(barrier, inc=1, device_id=p, device_id_type=MESH)

    me = slots[OWN]
    for h in range(2):
        kbuf[h, me, :, :HEAD] = pk_ref[:, h * HEAD : (h + 1) * HEAD]
        vbuf[h, me] = pv_ref[:, h * HEAD : (h + 1) * HEAD].T

    my_head = 0
    for h in range(8):
        my_head = my_head + jnp.where(slot_index_ref[h] == d, h, 0)
    odd = my_head % 2 == 1
    for i, ref in enumerate((sk_ref, sv_ref)):
        chosen = jnp.where(odd, ref[:, HEAD:], ref[:, :HEAD])
        for q in range(4):
            cand[q, i] = chosen[q * 64 : (q + 1) * 64]
        mine = pl.ds(pl.multiple_of(d * 32, 32), 32)
        for h in range(2):
            share[me, (2 * i + h) * 32 : (2 * i + h + 1) * 32, :] = ref[mine, h * HEAD : (h + 1) * HEAD]
    scat[t] = cand[t]
    for u in range(2):
        wide = dq_ref[u].astype(F32)
        for g in range(GROUP):
            at = (u * GROUP + g) * 4
            dq_rows[at : at + 4, :] = wide[:, g * HEAD : (g + 1) * HEAD]
    dqall[t] = dq_rows[...].astype(BF)

    pl.semaphore_wait(barrier, len(peers))

    def copy_k(h, which, to, n):
        s = slots[which]
        ref = kbuf.at[h, s, :, pl.ds(0, HEAD)]
        return remote(ref, ref, send_sem.at[h, n], recv_sem.at[h, s, 0], dev[to])

    def copy_v(h, which, to, n):
        s = slots[which]
        ref = vbuf.at[h, s]
        return remote(ref, ref, send_sem.at[h, n], recv_sem.at[h, s, 1], dev[to])

    pair_sends = [(OWN, 0, Z, 0), (OWN, 1, Z, 3)]
    x_sends = [(OWN, 0, L, 1), (OWN, 0, R, 2), (OWN, 1, L, 4), (OWN, 1, R, 5)]
    z_sends = [(Z, 0, L, 6), (Z, 0, R, 7), (Z, 1, L, 8), (Z, 1, R, 9)]
    forwards = {
        L: [(L, 0, R, 10)],
        R: [(R, 1, L, 11)],
        ZL: [(ZL, 0, R, 12)],
        ZR: [(ZR, 1, L, 13)],
        Z: z_sends,
    }

    def make(h, s):
        return (copy_v if s[1] else copy_k)(h, s[0], s[2], s[3])

    def start_all(h, sends):
        for s in sends:
            make(h, s).start()

    def arrive_one(h, which, kv):
        def go():
            (copy_v if kv else copy_k)(h, which, L, 0).wait_recv()
            start_all(h, [f for f in forwards.get(which, []) if f[1] == kv])

        when(exists(which), go)

    def arrive(h, which):
        arrive_one(h, which, 0)
        arrive_one(h, which, 1)

    def share_copy(buf, ss, rs, which, to, n):
        ref = buf.at[slots[which]]
        return remote(ref, ref, ss.at[n], rs.at[slots[which]], dev[to])

    stretch_share = functools.partial(share_copy, share, share_send, share_recv)
    slot_share = functools.partial(share_copy, slot_rows, slot_send, slot_recv)

    def send_share(copy):
        for n, to in enumerate((Z, L, R, O)):
            copy(OWN, to, n).start()

    def pass_share(copy):
        copy(Z, L, 0).wait_recv()
        for n, to in enumerate((L, R, O)):
            copy(Z, to, 4 + n).start()

    def take_share(copy):
        for which in (L, R, O, ZL, ZR, ZO):
            copy(which, L, 0).wait_recv()

    def share_done(copy):
        for n, to in enumerate((Z, L, R, O)):
            copy(OWN, to, n).wait_send()
        for n, to in enumerate((L, R, O)):
            copy(Z, to, 4 + n).wait_send()

    scat_copies = []
    dq_copies = []
    for i in range(3):
        q = (t + 1 + i) % 4
        cp = remote(cand.at[q], scat.at[t], scat_send.at[i], scat_recv.at[t], tp_peer[i])
        cp.start()
        scat_copies.append(cp)
        cp = remote(dqall.at[t], dqall.at[t], dq_send.at[i], dq_recv.at[t], tp_peer[i])
        cp.start()
        dq_copies.append(cp)

    q_rows = pl.ds(pl.multiple_of(d * 32, 32), 32)
    pair_copy = remote(q_ref.at[q_rows, pl.ds(8 * HEAD, 8 * HEAD)], q_pair, pair_sem.at[0], pair_sem.at[1], dev[Z])
    pair_copy.start()
    start_all(0, pair_sends)
    start_all(1, x_sends)
    start_all(0, x_sends)
    send_share(stretch_share)

    def q_copy(i):
        return remote(q_pair, q_all.at[d], q_send.at[i], q_recv.at[d], dec_peer[i])

    def spread_queries():
        pair_copy.wait_recv()
        for i in range(7):
            q_copy(i).start()
        q_all[d] = q_pair[...]

    def take_queries():
        for i in range(7):
            src = (d + 7 - i) % 8
            remote(q_pair, q_all.at[src], q_send.at[i], q_recv.at[src], dec_peer[i]).wait_recv()
        for g in range(8):
            qx[16 + g, :, :HEAD] = q_all[:, :, g * HEAD : (g + 1) * HEAD].reshape(ROWS, HEAD)

    one_lane = (lax.broadcasted_iota(jnp.int32, (ROWS, HEAD), 1) == 0).astype(F32).astype(BF)
    for j in range(24):
        if j < 16:
            qx[j, :, :HEAD] = q_ref[:, j * HEAD : (j + 1) * HEAD]
        qx[j, :, HEAD:] = one_lane
    m_ref[...] = jnp.full(m_ref.shape, NEG, F32)
    l_ref[...] = jnp.zeros(l_ref.shape, F32)
    acc_ref[...] = jnp.zeros(acc_ref.shape, F32)

    def score(h, slot, base, g, s_ref, x_ref):
        keys = kbuf[h, slot]
        for u in range(2):
            s = nt_dot(keys, qx[base + g * 2 + u])
            s_ref[u] = s
            x_ref[u] = jnp.max(s, axis=0, keepdims=True) * SCALE

    def update(j, s, top, vt):
        before = m_ref[j]
        now = jnp.maximum(before, top)
        p = jnp.exp2(s * SCALE - now)
        fade = jnp.exp2(before - now)
        l_ref[j] = l_ref[j] * fade + jnp.sum(p, axis=0, keepdims=True)
        m_ref[j] = now
        hi, lo = split(p)
        acc_ref[j] = acc_ref[j] * fade + (dot(vt, hi) + dot(vt, lo))

    def absorb(h, slot, base, g, s_ref, x_ref):
        for u in range(2):
            update(base + g * 2 + u, s_ref[u], x_ref[u], vbuf[h, slot])

    def flash_block(h, slot, base):
        score(h, slot, base, 0, s_a, x_a)
        score(h, slot, base, 1, s_b, x_b)
        absorb(h, slot, base, 0, s_a, x_a)
        score(h, slot, base, 2, s_a, x_a)
        absorb(h, slot, base, 1, s_b, x_b)
        score(h, slot, base, 3, s_b, x_b)
        absorb(h, slot, base, 2, s_a, x_a)
        absorb(h, slot, base, 3, s_b, x_b)

    def pick_slot_share():
        for cp in dq_copies + scat_copies:
            cp.wait_send()
        for i in range(3):
            src = (t + 3 - i) % 4
            remote(cand.at[0], scat.at[src], scat_send.at[i], scat_recv.at[src], tp_peer[i]).wait_recv()
        source = my_head // 2
        for i in range(2):
            quarter = scat[0, i]
            for q in range(1, 4):
                quarter = jnp.where(source == q, scat[q, i], quarter)
            slot_rows[me, 64 * i : 64 * i + 64, :] = quarter
        send_share(slot_share)

    def stretch_part():
        take_share(stretch_share)
        for h in range(2):
            kst[h] = share[:, h * 32 : (h + 1) * 32, :].reshape(ROWS, HEAD)
            vst[h] = share[:, 64 + h * 32 : 96 + h * 32, :].reshape(ROWS, HEAD).T
        kk = lax.broadcasted_iota(jnp.int32, (ROWS, ROWS), 0)
        key_row = (kk // 32) * ROWS + d * 32 + kk % 32
        query_row = c * ROWS + lax.broadcasted_iota(jnp.int32, (ROWS, ROWS), 1)
        usable = key_row <= query_row

        def stretch_score(h, g, s_ref, x_ref):
            for u in range(2):
                s = jnp.where(usable, nt_dot(kst[h], qx[h * 8 + g * 2 + u, :, :HEAD]), NEG)
                s_ref[u, :ROWS] = s
                x_ref[u] = jnp.max(s, axis=0, keepdims=True) * SCALE

        def stretch_absorb(h, g, s_ref, x_ref):
            for u in range(2):
                update(h * 8 + g * 2 + u, s_ref[u, :ROWS], x_ref[u], vst[h])

        def body(h, carry):
            stretch_score(h, 0, s_a, x_a)
            stretch_score(h, 1, s_b, x_b)
            stretch_absorb(h, 0, s_a, x_a)
            stretch_score(h, 2, s_a, x_a)
            stretch_absorb(h, 1, s_b, x_b)
            stretch_score(h, 3, s_b, x_b)
            stretch_absorb(h, 2, s_a, x_a)
            stretch_absorb(h, 3, s_b, x_b)
            return carry

        lax.fori_loop(0, 2, body, 0)

    def decode_cache():
        for cp in cache_copies:
            cp.wait()
        step_row = lax.broadcasted_iota(jnp.int32, (16, 1), 0) >= 8
        for r in range(4):
            qf = dq_rows[pl.ds(r, 16, stride=4), :]
            s = nt_dot(qf.astype(BF), ck[r]) * SCALE
            s = jnp.where(lax.broadcasted_iota(jnp.int32, (16, CACHE), 1) < lengths_ref[r], s, NEG)
            new = []
            for u in range(2):
                sn = jnp.sum(qf * dk_ref[u].astype(F32)[r : r + 1, :], axis=1, keepdims=True) * SCALE
                new.append(jnp.where(step_row, sn, NEG) if u else sn)
            top = jnp.maximum(jnp.max(s, axis=1, keepdims=True), jnp.maximum(new[0], new[1]))
            p = jnp.exp2(s - top)
            pn = [jnp.exp2(sn - top) for sn in new]
            total = jnp.sum(p, axis=1, keepdims=True) + pn[0] + pn[1]
            hi, lo = split(p)
            mixed = dot(jnp.concatenate([hi, lo], axis=0), cv[r])
            mixed = mixed[:16] + mixed[16:]
            for u in range(2):
                mixed = mixed + pn[u] * dv_ref[u].astype(F32)[r : r + 1, :]
            dec_o[pl.ds(r, 16, stride=4), :] = mixed / total
            dec_l[pl.ds(r, 16, stride=4), :] = jnp.broadcast_to(top + jnp.log2(total), (16, HEAD))

    dret_copies = [
        remote(dres.at[(t + 1 + i) % 4], dret.at[t], dret_send.at[i], dret_recv.at[t], tp_peer[i]) for i in range(3)
    ]

    def decode_stretch():
        take_share(slot_share)
        vslot[...] = slot_rows[:, 64:128, :].reshape(BLOCK, HEAD).T
        for i in range(3):
            src = (t + 3 - i) % 4
            remote(dqall.at[src], dqall.at[src], dq_send.at[i], dq_recv.at[src], tp_peer[i]).wait_recv()
        keys = slot_rows[:, 0:64, :].reshape(BLOCK, HEAD)
        s = nt_dot(keys, dqall[...].reshape(4 * 64, HEAD)) * SCALE
        top = jnp.max(s, axis=0, keepdims=True)
        p = jnp.exp2(s - top)
        total = jnp.sum(p, axis=0, keepdims=True)
        hi, lo = split(p)
        o = ((dot(vslot[...], hi) + dot(vslot[...], lo)) / total).T
        lse = jnp.broadcast_to(top + jnp.log2(total), (HEAD, 256)).T
        for q in range(4):
            dres[q, 0] = o[q * 64 : (q + 1) * 64]
            dres[q, 1] = lse[q * 64 : (q + 1) * 64]
        dret[t] = dres[t]
        for cp in dret_copies:
            cp.start()

    def decode_finish():
        for i in range(3):
            src = (t + 3 - i) % 4
            remote(dres.at[0], dret.at[src], dret_send.at[i], dret_recv.at[src], tp_peer[i]).wait_recv()
        top = dec_l[...]
        for q in range(4):
            top = jnp.maximum(top, dret[q, 1])
        w = jnp.exp2(dec_l[...] - top)
        num, den = w * dec_o[...], w
        for q in range(4):
            w = jnp.exp2(dret[q, 1] - top)
            num, den = num + w * dret[q, 0], den + w
        res = num / den
        for u in range(2):
            for g in range(GROUP):
                at = (u * GROUP + g) * 4
                dec_ref[u, :, g * HEAD : (g + 1) * HEAD] = res[at : at + 4, :].astype(BF)

    def core_copy(h):
        return remote(obuf.at[h, 1 - co], cbuf.at[h], core_send.at[h], core_recv.at[h], core_peer)

    def y_copy(h, i):
        return remote(
            obuf.at[h, co, (y + 1 + i) % 4], ybuf.at[h, y], y_send.at[h, i], y_recv.at[h, y], y_peer[i]
        )

    def finish_head(h):
        def body(g, carry):
            j = h * 8 + g
            o = (acc_ref[j] / l_ref[j]).T
            for k in range(8):
                obuf[h, k % 2, k // 2, g] = o[k * 32 : (k + 1) * 32]
            return carry

        lax.fori_loop(0, 8, body, 0)
        lse = [m_ref[h * 8 + g] + jnp.log2(l_ref[h * 8 + g]) for g in range(8)]
        lse = jnp.concatenate(lse + [jnp.zeros((120, ROWS), F32)], axis=0).T
        for k in range(8):
            obuf[h, k % 2, k // 2, 8] = lse[k * 32 : (k + 1) * 32]
        core_copy(h).start()

    def merge_cores(h):
        core_copy(h).wait_recv()

        def body(i, carry):
            a, b = obuf[h, co, i, 8], cbuf[h, i, 8]
            top = jnp.maximum(a, b)
            wa, wb = jnp.exp2(a - top), jnp.exp2(b - top)
            both = wa + wb
            obuf[h, co, i, 8] = top + jnp.log2(both)
            wa, wb = wa / both, wb / both
            for g in range(8):
                obuf[h, co, i, g] = obuf[h, co, i, g] * wa[:, g : g + 1] + cbuf[h, i, g] * wb[:, g : g + 1]
            return carry

        lax.fori_loop(0, 4, body, 0)
        for i in range(3):
            y_copy(h, i).start()

    def merge_y(h):
        for i in range(3):
            src = (y + 3 - i) % 4
            remote(
                obuf.at[h, co, 0], ybuf.at[h, src], y_send.at[h, i], y_recv.at[h, src], y_peer[i]
            ).wait_recv()
        ybuf[h, y] = obuf[h, co, y]
        parts = [ybuf.at[h, i] for i in range(4)]
        if h == 1:
            back_copy.wait_recv()
            parts.append(zbuf.at[1])
        lse = [p[8] for p in parts]
        top = functools.reduce(jnp.maximum, lse)
        w = [jnp.exp2(a - top) for a in lse]
        total = functools.reduce(jnp.add, w)
        inv = 1.0 / total
        w = [a * inv for a in w]
        if h == 2:
            zbuf[0, 8] = top + jnp.log2(total)
        for g in range(8):
            o = functools.reduce(jnp.add, [p[g] * a[:, g : g + 1] for p, a in zip(parts, w)])
            if h == 2:
                zbuf[0, g] = o
                continue
            out_ref[:, (h * 8 + g) * HEAD : (h * 8 + g + 1) * HEAD] = o.astype(BF)

    back_copy = remote(zbuf.at[0], zbuf.at[1], back_sem.at[0], back_sem.at[1], dev[Z])

    def send_back():
        merge_y(2)
        back_copy.start()

    ahead = {k: [] for k in range(16)}
    ahead[2] += [lambda: arrive(1, L), lambda: arrive(1, R), spread_queries]
    ahead[4] += [lambda: arrive(0, L), lambda: arrive(0, R), take_queries]
    ahead[5] += [lambda: arrive_one(0, Z, 0)]
    ahead[6] += [lambda: arrive_one(0, Z, 1), lambda: pass_share(stretch_share), pick_slot_share]
    ahead[7] += [lambda: arrive(1, O)]
    ahead[9] += [lambda: finish_head(2)]
    ahead[10] += [lambda: merge_cores(2)]
    ahead[11] += [lambda: arrive(0, ZL), lambda: arrive(0, ZR), lambda: arrive(0, O), stretch_part, lambda: finish_head(1)]
    ahead[12] += [lambda: merge_cores(1), lambda: pass_share(slot_share)]
    ahead[14] += [send_back]
    ahead[15] += [lambda: arrive(0, ZO)]

    def step(n, carry):
        h = 0
        slot = 0
        base = 0
        for k, (hk, which, rows) in enumerate(ORDER):
            if hk:
                h = h + jnp.where(n == k, 1, 0)
                base = base + jnp.where(n == k, 16 if rows == PAIR else 8, 0)
            slot = slot + jnp.where(n == k, slots[which], 0)
            if ahead[k]:

                def go(k=k):
                    for f in ahead[k]:
                        f()

                pl.when(n == k)(go)
        flash_block(h, slot, base)
        return carry

    lax.fori_loop(0, 16, step, 0)
    finish_head(0)
    decode_stretch()
    merge_cores(0)
    decode_cache()
    merge_y(1)
    decode_finish()
    merge_y(0)

    pair_copy.wait_send()
    back_copy.wait_send()
    for i in range(7):
        q_copy(i).wait_send()
    for h, sends in ((0, pair_sends), (0, x_sends), (1, x_sends)):
        for s in sends:
            make(h, s).wait_send()
    for which, sends in forwards.items():
        for h in range(2 if which in (L, R) else 1):
            for s in sends:
                make(h, s).wait_send()
    share_done(stretch_share)
    share_done(slot_share)
    for cp in dret_copies:
        cp.wait_send()
    for h in range(3):
        core_copy(h).wait_send()
        for i in range(3):
            y_copy(h, i).wait_send()


def fused(blocks, args):
    vmem = pl.BlockSpec(memory_space=pltpu.VMEM)
    smem = pl.BlockSpec(memory_space=pltpu.SMEM)
    anym = pl.BlockSpec(memory_space=pl.ANY)
    dma = pltpu.SemaphoreType.DMA
    return pl.pallas_call(
        functools.partial(kernel, blocks),
        out_shape=(
            jax.ShapeDtypeStruct((32, 2048), BF),
            jax.ShapeDtypeStruct((2, 4, GROUP * HEAD), BF),
        ),
        in_specs=[smem] * 3 + [vmem] * 8 + [anym] * 2,
        out_specs=(vmem, vmem),
        scratch_shapes=[
            pltpu.VMEM((4, CACHE, HEAD), BF),
            pltpu.VMEM((4, CACHE, HEAD), BF),
            pltpu.VMEM((24, ROWS, 2 * HEAD), BF),
            pltpu.VMEM((2, 8, BLOCK, 2 * HEAD), BF),
            pltpu.VMEM((2, 8, HEAD, BLOCK), BF),
            pltpu.VMEM((32, 8 * HEAD), BF),
            pltpu.VMEM((8, 32, 8 * HEAD), BF),
            pltpu.VMEM((8, 128, HEAD), BF),
            pltpu.VMEM((8, 128, HEAD), BF),
            pltpu.VMEM((4, 2, 64, HEAD), BF),
            pltpu.VMEM((4, 2, 64, HEAD), BF),
            pltpu.VMEM((64, HEAD), F32),
            pltpu.VMEM((4, 64, HEAD), BF),
            pltpu.VMEM((2, ROWS, HEAD), BF),
            pltpu.VMEM((2, HEAD, ROWS), BF),
            pltpu.VMEM((HEAD, BLOCK), BF),
            pltpu.VMEM((4, 2, 64, HEAD), F32),
            pltpu.VMEM((4, 2, 64, HEAD), F32),
            pltpu.VMEM((64, HEAD), F32),
            pltpu.VMEM((64, HEAD), F32),
            pltpu.VMEM((2, BLOCK, ROWS), F32),
            pltpu.VMEM((2, BLOCK, ROWS), F32),
            pltpu.VMEM((2, 1, ROWS), F32),
            pltpu.VMEM((2, 1, ROWS), F32),
            pltpu.VMEM((24, 1, ROWS), F32),
            pltpu.VMEM((24, 1, ROWS), F32),
            pltpu.VMEM((24, HEAD, ROWS), F32),
            pltpu.VMEM((3, 2, 4, 9, 32, HEAD), F32),
            pltpu.VMEM((3, 4, 9, 32, HEAD), F32),
            pltpu.VMEM((3, 4, 9, 32, HEAD), F32),
            pltpu.VMEM((2, 9, 32, HEAD), F32),
            dma((4, 2)),
            dma((2, 14)),
            dma((2, 8, 2)),
            dma((7,)),
            dma((8,)),
            dma((7,)),
            dma((8,)),
            dma((3,)),
            dma((4,)),
            dma((3,)),
            dma((4,)),
            dma((3,)),
            dma((4,)),
            dma((3,)),
            dma((3,)),
            dma((3, 3)),
            dma((3, 4)),
            dma((2,)),
            dma((7,)),
            dma((8,)),
            dma((2,)),
        ],
        compiler_params=pltpu.CompilerParams(
            collective_id=blocks, has_side_effects=True, vmem_limit_bytes=56 << 20
        ),
        name=f"attention_{blocks}",
    )(*args)


def shards(
    stretch_query_rows,
    stretch_key_rows,
    stretch_value_rows,
    prefix_key_rows,
    prefix_value_rows,
    offset,
    decode_query_rows,
    decode_keys,
    decode_value_rows,
    cache_keys,
    cached_value_rows,
    cache_lengths,
    head_slot_index,
):
    args = (
        offset,
        head_slot_index,
        cache_lengths,
        stretch_query_rows,
        prefix_key_rows,
        prefix_value_rows,
        stretch_key_rows,
        stretch_value_rows,
        decode_query_rows.reshape(2, 4, GROUP * HEAD),
        decode_keys.reshape(2, 4, HEAD),
        decode_value_rows.reshape(2, 4, HEAD),
        cache_keys.reshape(4, CACHE, HEAD),
        cached_value_rows.reshape(4, CACHE, HEAD),
    )
    prefill_out, dec = fused(8, args)
    return prefill_out, dec.reshape(2, 4, 1, GROUP * HEAD)


def solution(mesh):
    placed = (
        P("ctx", "tp"),
        P("ctx", "tp"),
        P("ctx", "tp"),
        P(("ctx", "dec"), "tp"),
        P(("ctx", "dec"), "tp"),
        P(),
        P(None, ("ctx", "tp"), "dec", None),
        P(None, ("ctx", "tp"), "dec", None),
        P(None, ("ctx", "tp"), "dec", None),
        P(("ctx", "tp"), "dec", None, None),
        P(("ctx", "tp"), "dec", None, None),
        P(("ctx", "tp")),
        P(),
    )
    return jax.shard_map(
        shards,
        mesh=mesh,
        in_specs=placed,
        out_specs=(P(("ctx", "dec"), "tp"), P(None, ("ctx", "tp"), "dec", None)),
        check_vma=False,
    )
```

```python
import functools

import jax
import jax.numpy as jnp
from jax import lax
from jax.experimental import pallas as pl
from jax.experimental.pallas import tpu as pltpu
from jax.sharding import PartitionSpec as P

HEAD = 128
GROUP = 8
BLOCK = 512
ROWS = 256
CACHE = 2048
NEG = -1e30
SCALE = HEAD**-0.5 * 1.4426950408889634
BF = jnp.bfloat16
F32 = jnp.float32
NT = (((1,), (1,)), ((), ()))
MESH = pl.DeviceIdType.MESH

OWN, L, R, O, Z, ZL, ZR, ZO = range(8)
MINE, PAIR = range(2)
ORDER = [
    (1, OWN, MINE),
    (0, OWN, MINE),
    (1, L, MINE),
    (1, R, MINE),
    (1, OWN, PAIR),
    (1, L, PAIR),
    (1, R, PAIR),
    (1, O, MINE),
    (1, O, PAIR),
    (0, L, MINE),
    (0, R, MINE),
    (0, O, MINE),
    (0, Z, MINE),
    (0, ZL, MINE),
    (0, ZR, MINE),
    (0, ZO, MINE),
]


def nt_dot(a, b):
    return lax.dot_general(a, b, NT, preferred_element_type=F32)


def dot(a, b):
    return jnp.dot(a, b, preferred_element_type=F32)


def split(p):
    hi = p.astype(BF)
    return hi, (p - hi.astype(F32)).astype(BF)


def kernel(
    blocks,
    offset_ref,
    slot_index_ref,
    lengths_ref,
    q_ref,
    pk_ref,
    pv_ref,
    sk_ref,
    sv_ref,
    dq_ref,
    dk_ref,
    dv_ref,
    ck_hbm,
    cv_hbm,
    out_ref,
    dec_ref,
    ck,
    cv,
    qx,
    kbuf,
    vbuf,
    q_pair,
    q_all,
    share,
    slot_rows,
    cand,
    scat,
    dq_rows,
    dqall,
    kst,
    vst,
    vslot,
    dres,
    dret,
    dec_o,
    dec_l,
    s_a,
    s_b,
    x_a,
    x_b,
    m_ref,
    l_ref,
    acc_ref,
    obuf,
    cbuf,
    ybuf,
    zbuf,
    cache_sem,
    send_sem,
    recv_sem,
    share_send,
    share_recv,
    slot_send,
    slot_recv,
    scat_send,
    scat_recv,
    dq_send,
    dq_recv,
    dret_send,
    dret_recv,
    core_send,
    core_recv,
    y_send,
    y_recv,
    pair_sem,
    q_send,
    q_recv,
    back_sem,
):
    c = lax.axis_index("ctx")
    t = lax.axis_index("tp")
    d = lax.axis_index("dec")
    zh, x = c // 4, c % 4
    y, co = d // 2, d % 2

    def ctx_at(dz, dx):
        return ((zh + dz) % 2) * 4 + (x + dx) % 4

    slots = {
        OWN: ctx_at(0, 0),
        L: ctx_at(0, 3),
        R: ctx_at(0, 1),
        O: ctx_at(0, 2),
        Z: ctx_at(1, 0),
        ZL: ctx_at(1, 3),
        ZR: ctx_at(1, 1),
        ZO: ctx_at(1, 2),
    }
    dev = {k: (slots[k], t, d) for k in (L, R, O, Z)}
    tp_peer = [(c, (t + i) % 4, d) for i in (1, 2, 3)]
    core_peer = (c, t, y * 2 + 1 - co)
    y_peer = [(c, t, ((y + i) % 4) * 2 + co) for i in (1, 2, 3)]
    dec_peer = [(c, t, (d + i) % 8) for i in range(1, 8)]

    def remote(src, dst, ss, rs, to):
        return pltpu.make_async_remote_copy(
            src_ref=src, dst_ref=dst, send_sem=ss, recv_sem=rs, device_id=to, device_id_type=MESH
        )

    def when(cond, f):
        if cond is True:
            f()
        else:
            pl.when(cond)(f)

    def exists(which):
        return True if blocks >= 8 else slots[which] < blocks

    cache_copies = []
    for r in range(4):
        for i, (hbm, vmem) in enumerate(((ck_hbm, ck), (cv_hbm, cv))):
            cp = pltpu.make_async_copy(hbm.at[r], vmem.at[r], cache_sem.at[r, i])
            cp.start()
            cache_copies.append(cp)

    row_id = lax.broadcasted_iota(jnp.int32, (BLOCK, HEAD), 0)
    lane_id = lax.broadcasted_iota(jnp.int32, (BLOCK, HEAD), 1)

    def fill(i, carry):
        limit = offset_ref[0] - (i * 8 + d) * BLOCK
        bias = jnp.where((lane_id == 0) & (row_id >= limit), NEG, 0.0).astype(BF)
        kbuf[0, i, :, HEAD:] = bias
        kbuf[1, i, :, HEAD:] = bias
        return carry

    lax.fori_loop(0, blocks, fill, 0)

    barrier = pltpu.get_barrier_semaphore()
    peers = [dev[L], dev[R], dev[O], dev[Z], *tp_peer, *dec_peer]
    for p in peers:
        pl.semaphore_signal(barrier, inc=1, device_id=p, device_id_type=MESH)

    me = slots[OWN]
    for h in range(2):
        kbuf[h, me, :, :HEAD] = pk_ref[:, h * HEAD : (h + 1) * HEAD]
        vbuf[h, me] = pv_ref[:, h * HEAD : (h + 1) * HEAD].T

    my_head = 0
    for h in range(8):
        my_head = my_head + jnp.where(slot_index_ref[h] == d, h, 0)
    odd = my_head % 2 == 1
    for i, ref in enumerate((sk_ref, sv_ref)):
        chosen = jnp.where(odd, ref[:, HEAD:], ref[:, :HEAD])
        for q in range(4):
            cand[q, i] = chosen[q * 64 : (q + 1) * 64]
        mine = pl.ds(pl.multiple_of(d * 32, 32), 32)
        for h in range(2):
            share[me, (2 * i + h) * 32 : (2 * i + h + 1) * 32, :] = ref[mine, h * HEAD : (h + 1) * HEAD]
    scat[t] = cand[t]
    for u in range(2):
        wide = dq_ref[u].astype(F32)
        for g in range(GROUP):
            at = (u * GROUP + g) * 4
            dq_rows[at : at + 4, :] = wide[:, g * HEAD : (g + 1) * HEAD]
    dqall[t] = dq_rows[...].astype(BF)

    one_lane = (lax.broadcasted_iota(jnp.int32, (ROWS, HEAD), 1) == 0).astype(F32).astype(BF)
    for j in range(24):
        if j < 16:
            qx[j, :, :HEAD] = q_ref[:, j * HEAD : (j + 1) * HEAD]
        qx[j, :, HEAD:] = one_lane
    m_ref[...] = jnp.full(m_ref.shape, NEG, F32)
    l_ref[...] = jnp.zeros(l_ref.shape, F32)
    acc_ref[...] = jnp.zeros(acc_ref.shape, F32)

    pl.semaphore_wait(barrier, len(peers))

    def copy_k(h, which, to, n):
        s = slots[which]
        ref = kbuf.at[h, s, :, pl.ds(0, HEAD)]
        return remote(ref, ref, send_sem.at[h, n], recv_sem.at[h, s, 0], dev[to])

    def copy_v(h, which, to, n):
        s = slots[which]
        ref = vbuf.at[h, s]
        return remote(ref, ref, send_sem.at[h, n], recv_sem.at[h, s, 1], dev[to])

    pair_sends = [(OWN, 0, Z, 0), (OWN, 1, Z, 3)]
    x_sends = [(OWN, 0, L, 1), (OWN, 0, R, 2), (OWN, 1, L, 4), (OWN, 1, R, 5)]
    z_sends = [(Z, 0, L, 6), (Z, 0, R, 7), (Z, 1, L, 8), (Z, 1, R, 9)]
    forwards = {
        L: [(L, 0, R, 10)],
        R: [(R, 1, L, 11)],
        ZL: [(ZL, 0, R, 12)],
        ZR: [(ZR, 1, L, 13)],
        Z: z_sends,
    }

    def make(h, s):
        return (copy_v if s[1] else copy_k)(h, s[0], s[2], s[3])

    def start_all(h, sends):
        for s in sends:
            make(h, s).start()

    def arrive_one(h, which, kv):
        def go():
            (copy_v if kv else copy_k)(h, which, L, 0).wait_recv()
            start_all(h, [f for f in forwards.get(which, []) if f[1] == kv])

        when(exists(which), go)

    def arrive(h, which):
        arrive_one(h, which, 0)
        arrive_one(h, which, 1)

    def share_copy(buf, ss, rs, which, to, n):
        ref = buf.at[slots[which]]
        return remote(ref, ref, ss.at[n], rs.at[slots[which]], dev[to])

    stretch_share = functools.partial(share_copy, share, share_send, share_recv)
    slot_share = functools.partial(share_copy, slot_rows, slot_send, slot_recv)

    def send_share(copy):
        for n, to in enumerate((Z, L, R, O)):
            copy(OWN, to, n).start()

    def pass_share(copy):
        copy(Z, L, 0).wait_recv()
        for n, to in enumerate((L, R, O)):
            copy(Z, to, 4 + n).start()

    def take_share(copy):
        for which in (L, R, O, ZL, ZR, ZO):
            copy(which, L, 0).wait_recv()

    def share_done(copy):
        for n, to in enumerate((Z, L, R, O)):
            copy(OWN, to, n).wait_send()
        for n, to in enumerate((L, R, O)):
            copy(Z, to, 4 + n).wait_send()

    scat_copies = []
    dq_copies = []
    for i in range(3):
        q = (t + 1 + i) % 4
        cp = remote(cand.at[q], scat.at[t], scat_send.at[i], scat_recv.at[t], tp_peer[i])
        cp.start()
        scat_copies.append(cp)
        cp = remote(dqall.at[t], dqall.at[t], dq_send.at[i], dq_recv.at[t], tp_peer[i])
        cp.start()
        dq_copies.append(cp)

    q_rows = pl.ds(pl.multiple_of(d * 32, 32), 32)
    pair_copy = remote(q_ref.at[q_rows, pl.ds(8 * HEAD, 8 * HEAD)], q_pair, pair_sem.at[0], pair_sem.at[1], dev[Z])
    pair_copy.start()
    start_all(0, pair_sends)
    start_all(1, x_sends)
    start_all(0, x_sends)
    send_share(stretch_share)

    def q_copy(i):
        return remote(q_pair, q_all.at[d], q_send.at[i], q_recv.at[d], dec_peer[i])

    def spread_queries():
        pair_copy.wait_recv()
        for i in range(7):
            q_copy(i).start()
        q_all[d] = q_pair[...]

    def take_queries():
        for i in range(7):
            src = (d + 7 - i) % 8
            remote(q_pair, q_all.at[src], q_send.at[i], q_recv.at[src], dec_peer[i]).wait_recv()
        for g in range(8):
            qx[16 + g, :, :HEAD] = q_all[:, :, g * HEAD : (g + 1) * HEAD].reshape(ROWS, HEAD)

    def score(h, slot, base, g, s_ref, x_ref):
        keys = kbuf[h, slot]
        for u in range(2):
            s = nt_dot(keys, qx[base + g * 2 + u])
            s_ref[u] = s
            x_ref[u] = jnp.max(s, axis=0, keepdims=True) * SCALE

    def update(j, s, top, vt):
        before = m_ref[j]
        now = jnp.maximum(before, top)
        p = jnp.exp2(s * SCALE - now)
        fade = jnp.exp2(before - now)
        l_ref[j] = l_ref[j] * fade + jnp.sum(p, axis=0, keepdims=True)
        m_ref[j] = now
        hi, lo = split(p)
        acc_ref[j] = acc_ref[j] * fade + (dot(vt, hi) + dot(vt, lo))

    def absorb(h, slot, base, g, s_ref, x_ref):
        for u in range(2):
            update(base + g * 2 + u, s_ref[u], x_ref[u], vbuf[h, slot])

    def flash_block(h, slot, base):
        def score_one(g):
            s = nt_dot(kbuf[h, slot], qx[base + g])
            s_ref, x_ref = (s_a, x_a) if g % 4 < 2 else (s_b, x_b)
            s_ref[g % 2] = s
            x_ref[g % 2] = jnp.max(s, axis=0, keepdims=True) * SCALE

        def absorb_one(g):
            s_ref, x_ref = (s_a, x_a) if g % 4 < 2 else (s_b, x_b)
            update(base + g, s_ref[g % 2], x_ref[g % 2], vbuf[h, slot])

        for g in range(3):
            score_one(g)
        for g in range(8):
            absorb_one(g)
            if g + 3 < 8:
                score_one(g + 3)

    def pick_slot_share():
        for cp in dq_copies + scat_copies:
            cp.wait_send()
        for i in range(3):
            src = (t + 3 - i) % 4
            remote(cand.at[0], scat.at[src], scat_send.at[i], scat_recv.at[src], tp_peer[i]).wait_recv()
        source = my_head // 2
        for i in range(2):
            quarter = scat[0, i]
            for q in range(1, 4):
                quarter = jnp.where(source == q, scat[q, i], quarter)
            slot_rows[me, 64 * i : 64 * i + 64, :] = quarter
        send_share(slot_share)

    def stretch_part():
        take_share(stretch_share)
        for h in range(2):
            kst[h] = share[:, h * 32 : (h + 1) * 32, :].reshape(ROWS, HEAD)
            vst[h] = share[:, 64 + h * 32 : 96 + h * 32, :].reshape(ROWS, HEAD).T
        kk = lax.broadcasted_iota(jnp.int32, (ROWS, ROWS), 0)
        key_row = (kk // 32) * ROWS + d * 32 + kk % 32
        query_row = c * ROWS + lax.broadcasted_iota(jnp.int32, (ROWS, ROWS), 1)
        usable = key_row <= query_row

        def stretch_score(h, g, s_ref, x_ref):
            for u in range(2):
                s = jnp.where(usable, nt_dot(kst[h], qx[h * 8 + g * 2 + u, :, :HEAD]), NEG)
                s_ref[u, :ROWS] = s
                x_ref[u] = jnp.max(s, axis=0, keepdims=True) * SCALE

        def stretch_absorb(h, g, s_ref, x_ref):
            for u in range(2):
                update(h * 8 + g * 2 + u, s_ref[u, :ROWS], x_ref[u], vst[h])

        def body(h, carry):
            stretch_score(h, 0, s_a, x_a)
            stretch_score(h, 1, s_b, x_b)
            stretch_absorb(h, 0, s_a, x_a)
            stretch_score(h, 2, s_a, x_a)
            stretch_absorb(h, 1, s_b, x_b)
            stretch_score(h, 3, s_b, x_b)
            stretch_absorb(h, 2, s_a, x_a)
            stretch_absorb(h, 3, s_b, x_b)
            return carry

        lax.fori_loop(0, 2, body, 0)

    def decode_cache():
        for cp in cache_copies:
            cp.wait()
        step_row = lax.broadcasted_iota(jnp.int32, (16, 1), 0) >= 8
        for r in range(4):
            qf = dq_rows[pl.ds(r, 16, stride=4), :]
            s = nt_dot(qf.astype(BF), ck[r]) * SCALE
            s = jnp.where(lax.broadcasted_iota(jnp.int32, (16, CACHE), 1) < lengths_ref[r], s, NEG)
            new = []
            for u in range(2):
                sn = jnp.sum(qf * dk_ref[u].astype(F32)[r : r + 1, :], axis=1, keepdims=True) * SCALE
                new.append(jnp.where(step_row, sn, NEG) if u else sn)
            top = jnp.maximum(jnp.max(s, axis=1, keepdims=True), jnp.maximum(new[0], new[1]))
            p = jnp.exp2(s - top)
            pn = [jnp.exp2(sn - top) for sn in new]
            total = jnp.sum(p, axis=1, keepdims=True) + pn[0] + pn[1]
            hi, lo = split(p)
            mixed = dot(jnp.concatenate([hi, lo], axis=0), cv[r])
            mixed = mixed[:16] + mixed[16:]
            for u in range(2):
                mixed = mixed + pn[u] * dv_ref[u].astype(F32)[r : r + 1, :]
            dec_o[pl.ds(r, 16, stride=4), :] = mixed / total
            dec_l[pl.ds(r, 16, stride=4), :] = jnp.broadcast_to(top + jnp.log2(total), (16, HEAD))

    dret_copies = [
        remote(dres.at[(t + 1 + i) % 4], dret.at[t], dret_send.at[i], dret_recv.at[t], tp_peer[i]) for i in range(3)
    ]

    def decode_stretch():
        take_share(slot_share)
        vslot[...] = slot_rows[:, 64:128, :].reshape(BLOCK, HEAD).T
        for i in range(3):
            src = (t + 3 - i) % 4
            remote(dqall.at[src], dqall.at[src], dq_send.at[i], dq_recv.at[src], tp_peer[i]).wait_recv()
        keys = slot_rows[:, 0:64, :].reshape(BLOCK, HEAD)
        s = nt_dot(keys, dqall[...].reshape(4 * 64, HEAD)) * SCALE
        top = jnp.max(s, axis=0, keepdims=True)
        p = jnp.exp2(s - top)
        total = jnp.sum(p, axis=0, keepdims=True)
        hi, lo = split(p)
        o = ((dot(vslot[...], hi) + dot(vslot[...], lo)) / total).T
        lse = jnp.broadcast_to(top + jnp.log2(total), (HEAD, 256)).T
        for q in range(4):
            dres[q, 0] = o[q * 64 : (q + 1) * 64]
            dres[q, 1] = lse[q * 64 : (q + 1) * 64]
        dret[t] = dres[t]
        for cp in dret_copies:
            cp.start()

    def decode_finish():
        for i in range(3):
            src = (t + 3 - i) % 4
            remote(dres.at[0], dret.at[src], dret_send.at[i], dret_recv.at[src], tp_peer[i]).wait_recv()
        top = dec_l[...]
        for q in range(4):
            top = jnp.maximum(top, dret[q, 1])
        w = jnp.exp2(dec_l[...] - top)
        num, den = w * dec_o[...], w
        for q in range(4):
            w = jnp.exp2(dret[q, 1] - top)
            num, den = num + w * dret[q, 0], den + w
        res = num / den
        for u in range(2):
            for g in range(GROUP):
                at = (u * GROUP + g) * 4
                dec_ref[u, :, g * HEAD : (g + 1) * HEAD] = res[at : at + 4, :].astype(BF)

    def core_copy(h):
        return remote(obuf.at[h, 1 - co], cbuf.at[h], core_send.at[h], core_recv.at[h], core_peer)

    def y_copy(h, i):
        return remote(
            obuf.at[h, co, (y + 1 + i) % 4], ybuf.at[h, y], y_send.at[h, i], y_recv.at[h, y], y_peer[i]
        )

    def finish_head(h):
        def body(g, carry):
            j = h * 8 + g
            o = (acc_ref[j] / l_ref[j]).T
            for k in range(8):
                obuf[h, k % 2, k // 2, g] = o[k * 32 : (k + 1) * 32]
            return carry

        lax.fori_loop(0, 8, body, 0)
        lse = [m_ref[h * 8 + g] + jnp.log2(l_ref[h * 8 + g]) for g in range(8)]
        lse = jnp.concatenate(lse + [jnp.zeros((120, ROWS), F32)], axis=0).T
        for k in range(8):
            obuf[h, k % 2, k // 2, 8] = lse[k * 32 : (k + 1) * 32]
        core_copy(h).start()

    def merge_cores(h):
        core_copy(h).wait_recv()

        def body(i, carry):
            a, b = obuf[h, co, i, 8], cbuf[h, i, 8]
            top = jnp.maximum(a, b)
            wa, wb = jnp.exp2(a - top), jnp.exp2(b - top)
            both = wa + wb
            obuf[h, co, i, 8] = top + jnp.log2(both)
            wa, wb = wa / both, wb / both
            for g in range(8):
                obuf[h, co, i, g] = obuf[h, co, i, g] * wa[:, g : g + 1] + cbuf[h, i, g] * wb[:, g : g + 1]
            return carry

        lax.fori_loop(0, 4, body, 0)
        for i in range(3):
            y_copy(h, i).start()

    def merge_y(h):
        for i in range(3):
            src = (y + 3 - i) % 4
            remote(
                obuf.at[h, co, 0], ybuf.at[h, src], y_send.at[h, i], y_recv.at[h, src], y_peer[i]
            ).wait_recv()
        ybuf[h, y] = obuf[h, co, y]
        parts = [ybuf.at[h, i] for i in range(4)]
        if h == 1:
            back_copy.wait_recv()
            parts.append(zbuf.at[1])
        lse = [p[8] for p in parts]
        top = functools.reduce(jnp.maximum, lse)
        w = [jnp.exp2(a - top) for a in lse]
        total = functools.reduce(jnp.add, w)
        inv = 1.0 / total
        w = [a * inv for a in w]
        if h == 2:
            zbuf[0, 8] = top + jnp.log2(total)
        for g in range(8):
            o = functools.reduce(jnp.add, [p[g] * a[:, g : g + 1] for p, a in zip(parts, w)])
            if h == 2:
                zbuf[0, g] = o
                continue
            out_ref[:, (h * 8 + g) * HEAD : (h * 8 + g + 1) * HEAD] = o.astype(BF)

    back_copy = remote(zbuf.at[0], zbuf.at[1], back_sem.at[0], back_sem.at[1], dev[Z])

    def send_back():
        merge_y(2)
        back_copy.start()

    ahead = {k: [] for k in range(16)}
    ahead[2] += [lambda: arrive(1, L), lambda: arrive(1, R), spread_queries]
    ahead[4] += [lambda: arrive(0, L), lambda: arrive(0, R), take_queries]
    ahead[5] += [lambda: arrive_one(0, Z, 0)]
    ahead[6] += [lambda: arrive_one(0, Z, 1), lambda: pass_share(stretch_share), pick_slot_share]
    ahead[7] += [lambda: arrive(1, O)]
    ahead[9] += [lambda: finish_head(2)]
    ahead[10] += [lambda: merge_cores(2)]
    ahead[11] += [lambda: arrive(0, ZL), lambda: arrive(0, ZR), lambda: arrive(0, O), stretch_part, lambda: finish_head(1)]
    ahead[12] += [lambda: merge_cores(1), lambda: pass_share(slot_share)]
    ahead[14] += [send_back]
    ahead[15] += [lambda: arrive(0, ZO)]

    def step(n, carry):
        h = 0
        slot = 0
        base = 0
        for k, (hk, which, rows) in enumerate(ORDER):
            if hk:
                h = h + jnp.where(n == k, 1, 0)
                base = base + jnp.where(n == k, 16 if rows == PAIR else 8, 0)
            slot = slot + jnp.where(n == k, slots[which], 0)
            if ahead[k]:

                def go(k=k):
                    for f in ahead[k]:
                        f()

                pl.when(n == k)(go)
        flash_block(h, slot, base)
        return carry

    lax.fori_loop(0, 16, step, 0)
    finish_head(0)
    decode_stretch()
    merge_cores(0)
    decode_cache()
    merge_y(1)
    decode_finish()
    merge_y(0)

    pair_copy.wait_send()
    back_copy.wait_send()
    for i in range(7):
        q_copy(i).wait_send()
    for h, sends in ((0, pair_sends), (0, x_sends), (1, x_sends)):
        for s in sends:
            make(h, s).wait_send()
    for which, sends in forwards.items():
        for h in range(2 if which in (L, R) else 1):
            for s in sends:
                make(h, s).wait_send()
    share_done(stretch_share)
    share_done(slot_share)
    for cp in dret_copies:
        cp.wait_send()
    for h in range(3):
        core_copy(h).wait_send()
        for i in range(3):
            y_copy(h, i).wait_send()


def fused(blocks, args):
    vmem = pl.BlockSpec(memory_space=pltpu.VMEM)
    smem = pl.BlockSpec(memory_space=pltpu.SMEM)
    anym = pl.BlockSpec(memory_space=pl.ANY)
    dma = pltpu.SemaphoreType.DMA
    return pl.pallas_call(
        functools.partial(kernel, blocks),
        out_shape=(
            jax.ShapeDtypeStruct((32, 2048), BF),
            jax.ShapeDtypeStruct((2, 4, GROUP * HEAD), BF),
        ),
        in_specs=[smem] * 3 + [vmem] * 8 + [anym] * 2,
        out_specs=(vmem, vmem),
        scratch_shapes=[
            pltpu.VMEM((4, CACHE, HEAD), BF),
            pltpu.VMEM((4, CACHE, HEAD), BF),
            pltpu.VMEM((24, ROWS, 2 * HEAD), BF),
            pltpu.VMEM((2, 8, BLOCK, 2 * HEAD), BF),
            pltpu.VMEM((2, 8, HEAD, BLOCK), BF),
            pltpu.VMEM((32, 8 * HEAD), BF),
            pltpu.VMEM((8, 32, 8 * HEAD), BF),
            pltpu.VMEM((8, 128, HEAD), BF),
            pltpu.VMEM((8, 128, HEAD), BF),
            pltpu.VMEM((4, 2, 64, HEAD), BF),
            pltpu.VMEM((4, 2, 64, HEAD), BF),
            pltpu.VMEM((64, HEAD), F32),
            pltpu.VMEM((4, 64, HEAD), BF),
            pltpu.VMEM((2, ROWS, HEAD), BF),
            pltpu.VMEM((2, HEAD, ROWS), BF),
            pltpu.VMEM((HEAD, BLOCK), BF),
            pltpu.VMEM((4, 2, 64, HEAD), F32),
            pltpu.VMEM((4, 2, 64, HEAD), F32),
            pltpu.VMEM((64, HEAD), F32),
            pltpu.VMEM((64, HEAD), F32),
            pltpu.VMEM((2, BLOCK, ROWS), F32),
            pltpu.VMEM((2, BLOCK, ROWS), F32),
            pltpu.VMEM((2, 1, ROWS), F32),
            pltpu.VMEM((2, 1, ROWS), F32),
            pltpu.VMEM((24, 1, ROWS), F32),
            pltpu.VMEM((24, 1, ROWS), F32),
            pltpu.VMEM((24, HEAD, ROWS), F32),
            pltpu.VMEM((3, 2, 4, 9, 32, HEAD), F32),
            pltpu.VMEM((3, 4, 9, 32, HEAD), F32),
            pltpu.VMEM((3, 4, 9, 32, HEAD), F32),
            pltpu.VMEM((2, 9, 32, HEAD), F32),
            dma((4, 2)),
            dma((2, 14)),
            dma((2, 8, 2)),
            dma((7,)),
            dma((8,)),
            dma((7,)),
            dma((8,)),
            dma((3,)),
            dma((4,)),
            dma((3,)),
            dma((4,)),
            dma((3,)),
            dma((4,)),
            dma((3,)),
            dma((3,)),
            dma((3, 3)),
            dma((3, 4)),
            dma((2,)),
            dma((7,)),
            dma((8,)),
            dma((2,)),
        ],
        compiler_params=pltpu.CompilerParams(
            collective_id=blocks, has_side_effects=True, vmem_limit_bytes=56 << 20
        ),
        name=f"attention_{blocks}",
    )(*args)


def shards(
    stretch_query_rows,
    stretch_key_rows,
    stretch_value_rows,
    prefix_key_rows,
    prefix_value_rows,
    offset,
    decode_query_rows,
    decode_keys,
    decode_value_rows,
    cache_keys,
    cached_value_rows,
    cache_lengths,
    head_slot_index,
):
    args = (
        offset,
        head_slot_index,
        cache_lengths,
        stretch_query_rows,
        prefix_key_rows,
        prefix_value_rows,
        stretch_key_rows,
        stretch_value_rows,
        decode_query_rows.reshape(2, 4, GROUP * HEAD),
        decode_keys.reshape(2, 4, HEAD),
        decode_value_rows.reshape(2, 4, HEAD),
        cache_keys.reshape(4, CACHE, HEAD),
        cached_value_rows.reshape(4, CACHE, HEAD),
    )
    prefill_out, dec = fused(8, args)
    return prefill_out, dec.reshape(2, 4, 1, GROUP * HEAD)


def solution(mesh):
    placed = (
        P("ctx", "tp"),
        P("ctx", "tp"),
        P("ctx", "tp"),
        P(("ctx", "dec"), "tp"),
        P(("ctx", "dec"), "tp"),
        P(),
        P(None, ("ctx", "tp"), "dec", None),
        P(None, ("ctx", "tp"), "dec", None),
        P(None, ("ctx", "tp"), "dec", None),
        P(("ctx", "tp"), "dec", None, None),
        P(("ctx", "tp"), "dec", None, None),
        P(("ctx", "tp")),
        P(),
    )
    return jax.shard_map(
        shards,
        mesh=mesh,
        in_specs=placed,
        out_specs=(P(("ctx", "dec"), "tp"), P(None, ("ctx", "tp"), "dec", None)),
        check_vma=False,
    )
```

```python
import functools

import jax
import jax.numpy as jnp
from jax import lax
from jax.experimental import pallas as pl
from jax.experimental.pallas import tpu as pltpu
from jax.sharding import PartitionSpec as P

HEAD = 128
GROUP = 8
BLOCK = 512
ROWS = 256
CACHE = 2048
NEG = -1e30
SCALE = HEAD**-0.5 * 1.4426950408889634
BF = jnp.bfloat16
F32 = jnp.float32
NT = (((1,), (1,)), ((), ()))
MESH = pl.DeviceIdType.MESH

OWN, L, R, O, Z, ZL, ZR, ZO = range(8)
MINE, PAIR = range(2)
ORDER = [
    (1, OWN, MINE),
    (0, OWN, MINE),
    (1, L, MINE),
    (1, R, MINE),
    (1, OWN, PAIR),
    (1, L, PAIR),
    (1, R, PAIR),
    (1, O, MINE),
    (1, O, PAIR),
    (0, L, MINE),
    (0, R, MINE),
    (0, O, MINE),
    (0, Z, MINE),
    (0, ZL, MINE),
    (0, ZR, MINE),
    (0, ZO, MINE),
]


def nt_dot(a, b):
    return lax.dot_general(a, b, NT, preferred_element_type=F32)


def dot(a, b):
    return jnp.dot(a, b, preferred_element_type=F32)


def split(p):
    hi = p.astype(BF)
    return hi, (p - hi.astype(F32)).astype(BF)


def kernel(
    blocks,
    offset_ref,
    slot_index_ref,
    lengths_ref,
    q_ref,
    pk_ref,
    pv_ref,
    sk_ref,
    sv_ref,
    dq_ref,
    dk_ref,
    dv_ref,
    ck_hbm,
    cv_hbm,
    out_ref,
    dec_ref,
    ck,
    cv,
    qx,
    kbuf,
    vbuf,
    q_pair,
    q_all,
    share,
    slot_rows,
    cand,
    scat,
    dq_rows,
    dqall,
    kst,
    vst,
    vslot,
    dres,
    dret,
    dec_o,
    dec_l,
    s_a,
    s_b,
    x_a,
    x_b,
    m_ref,
    l_ref,
    acc_ref,
    obuf,
    cbuf,
    ybuf,
    zbuf,
    cache_sem,
    send_sem,
    recv_sem,
    share_send,
    share_recv,
    slot_send,
    slot_recv,
    scat_send,
    scat_recv,
    dq_send,
    dq_recv,
    dret_send,
    dret_recv,
    core_send,
    core_recv,
    y_send,
    y_recv,
    pair_sem,
    q_send,
    q_recv,
    back_sem,
):
    c = lax.axis_index("ctx")
    t = lax.axis_index("tp")
    d = lax.axis_index("dec")
    zh, x = c // 4, c % 4
    y, co = d // 2, d % 2

    def ctx_at(dz, dx):
        return ((zh + dz) % 2) * 4 + (x + dx) % 4

    slots = {
        OWN: ctx_at(0, 0),
        L: ctx_at(0, 3),
        R: ctx_at(0, 1),
        O: ctx_at(0, 2),
        Z: ctx_at(1, 0),
        ZL: ctx_at(1, 3),
        ZR: ctx_at(1, 1),
        ZO: ctx_at(1, 2),
    }
    dev = {k: (slots[k], t, d) for k in (L, R, O, Z)}
    tp_peer = [(c, (t + i) % 4, d) for i in (1, 2, 3)]
    core_peer = (c, t, y * 2 + 1 - co)
    y_peer = [(c, t, ((y + i) % 4) * 2 + co) for i in (1, 2, 3)]
    dec_peer = [(c, t, (d + i) % 8) for i in range(1, 8)]

    def remote(src, dst, ss, rs, to):
        return pltpu.make_async_remote_copy(
            src_ref=src, dst_ref=dst, send_sem=ss, recv_sem=rs, device_id=to, device_id_type=MESH
        )

    def when(cond, f):
        if cond is True:
            f()
        else:
            pl.when(cond)(f)

    def exists(which):
        return True if blocks >= 8 else slots[which] < blocks

    cache_copies = []
    for r in range(4):
        for i, (hbm, vmem) in enumerate(((ck_hbm, ck), (cv_hbm, cv))):
            cp = pltpu.make_async_copy(hbm.at[r], vmem.at[r], cache_sem.at[r, i])
            cp.start()
            cache_copies.append(cp)

    row_id = lax.broadcasted_iota(jnp.int32, (BLOCK, HEAD), 0)
    lane_id = lax.broadcasted_iota(jnp.int32, (BLOCK, HEAD), 1)

    def fill(i, carry):
        limit = offset_ref[0] - (i * 8 + d) * BLOCK
        bias = jnp.where((lane_id == 0) & (row_id >= limit), NEG, 0.0).astype(BF)
        kbuf[0, i, :, HEAD:] = bias
        kbuf[1, i, :, HEAD:] = bias
        return carry

    lax.fori_loop(0, blocks, fill, 0)

    barrier = pltpu.get_barrier_semaphore()
    peers = [dev[L], dev[R], dev[O], dev[Z], *tp_peer, *dec_peer]
    for p in peers:
        pl.semaphore_signal(barrier, inc=1, device_id=p, device_id_type=MESH)

    me = slots[OWN]
    for h in range(2):
        kbuf[h, me, :, :HEAD] = pk_ref[:, h * HEAD : (h + 1) * HEAD]
        vbuf[h, me] = pv_ref[:, h * HEAD : (h + 1) * HEAD].T

    my_head = 0
    for h in range(8):
        my_head = my_head + jnp.where(slot_index_ref[h] == d, h, 0)
    odd = my_head % 2 == 1
    for i, ref in enumerate((sk_ref, sv_ref)):
        chosen = jnp.where(odd, ref[:, HEAD:], ref[:, :HEAD])
        for q in range(4):
            cand[q, i] = chosen[q * 64 : (q + 1) * 64]
        mine = pl.ds(pl.multiple_of(d * 32, 32), 32)
        for h in range(2):
            share[me, (2 * i + h) * 32 : (2 * i + h + 1) * 32, :] = ref[mine, h * HEAD : (h + 1) * HEAD]
    scat[t] = cand[t]
    for u in range(2):
        wide = dq_ref[u].astype(F32)
        for g in range(GROUP):
            at = (u * GROUP + g) * 4
            dq_rows[at : at + 4, :] = wide[:, g * HEAD : (g + 1) * HEAD]
    dqall[t] = dq_rows[...].astype(BF)

    one_lane = (lax.broadcasted_iota(jnp.int32, (ROWS, HEAD), 1) == 0).astype(F32).astype(BF)
    for j in range(24):
        if j < 16:
            qx[j, :, :HEAD] = q_ref[:, j * HEAD : (j + 1) * HEAD]
        qx[j, :, HEAD:] = one_lane
    m_ref[...] = jnp.full(m_ref.shape, NEG, F32)
    l_ref[...] = jnp.zeros(l_ref.shape, F32)
    acc_ref[...] = jnp.zeros(acc_ref.shape, F32)

    pl.semaphore_wait(barrier, len(peers))

    def copy_k(h, which, to, n):
        s = slots[which]
        ref = kbuf.at[h, s, :, pl.ds(0, HEAD)]
        return remote(ref, ref, send_sem.at[h, n], recv_sem.at[h, s, 0], dev[to])

    def copy_v(h, which, to, n):
        s = slots[which]
        ref = vbuf.at[h, s]
        return remote(ref, ref, send_sem.at[h, n], recv_sem.at[h, s, 1], dev[to])

    pair_sends = [(OWN, 0, Z, 0), (OWN, 1, Z, 3)]
    x_sends = [(OWN, 0, L, 1), (OWN, 0, R, 2), (OWN, 1, L, 4), (OWN, 1, R, 5)]
    z_sends = [(Z, 0, L, 6), (Z, 0, R, 7), (Z, 1, L, 8), (Z, 1, R, 9)]
    forwards = {
        L: [(L, 0, R, 10)],
        R: [(R, 1, L, 11)],
        ZL: [(ZL, 0, R, 12)],
        ZR: [(ZR, 1, L, 13)],
        Z: z_sends,
    }

    def make(h, s):
        return (copy_v if s[1] else copy_k)(h, s[0], s[2], s[3])

    def start_all(h, sends):
        for s in sends:
            make(h, s).start()

    def arrive_one(h, which, kv):
        def go():
            (copy_v if kv else copy_k)(h, which, L, 0).wait_recv()
            start_all(h, [f for f in forwards.get(which, []) if f[1] == kv])

        when(exists(which), go)

    def arrive(h, which):
        arrive_one(h, which, 0)
        arrive_one(h, which, 1)

    def share_copy(buf, ss, rs, which, to, n):
        ref = buf.at[slots[which]]
        return remote(ref, ref, ss.at[n], rs.at[slots[which]], dev[to])

    stretch_share = functools.partial(share_copy, share, share_send, share_recv)
    slot_share = functools.partial(share_copy, slot_rows, slot_send, slot_recv)

    def send_share(copy):
        for n, to in enumerate((Z, L, R, O)):
            copy(OWN, to, n).start()

    def pass_share(copy):
        copy(Z, L, 0).wait_recv()
        for n, to in enumerate((L, R, O)):
            copy(Z, to, 4 + n).start()

    def take_share(copy):
        for which in (L, R, O, ZL, ZR, ZO):
            copy(which, L, 0).wait_recv()

    def share_done(copy):
        for n, to in enumerate((Z, L, R, O)):
            copy(OWN, to, n).wait_send()
        for n, to in enumerate((L, R, O)):
            copy(Z, to, 4 + n).wait_send()

    scat_copies = []
    dq_copies = []
    for i in range(3):
        q = (t + 1 + i) % 4
        cp = remote(cand.at[q], scat.at[t], scat_send.at[i], scat_recv.at[t], tp_peer[i])
        cp.start()
        scat_copies.append(cp)
        cp = remote(dqall.at[t], dqall.at[t], dq_send.at[i], dq_recv.at[t], tp_peer[i])
        cp.start()
        dq_copies.append(cp)

    q_rows = pl.ds(pl.multiple_of(d * 32, 32), 32)
    pair_copy = remote(q_ref.at[q_rows, pl.ds(8 * HEAD, 8 * HEAD)], q_pair, pair_sem.at[0], pair_sem.at[1], dev[Z])
    pair_copy.start()
    start_all(0, pair_sends)
    start_all(1, x_sends)
    start_all(0, x_sends)
    send_share(stretch_share)

    def q_copy(i):
        return remote(q_pair, q_all.at[d], q_send.at[i], q_recv.at[d], dec_peer[i])

    def spread_queries():
        pair_copy.wait_recv()
        for i in range(7):
            q_copy(i).start()
        q_all[d] = q_pair[...]

    def take_queries():
        for i in range(7):
            src = (d + 7 - i) % 8
            remote(q_pair, q_all.at[src], q_send.at[i], q_recv.at[src], dec_peer[i]).wait_recv()
        for g in range(8):
            qx[16 + g, :, :HEAD] = q_all[:, :, g * HEAD : (g + 1) * HEAD].reshape(ROWS, HEAD)

    def score(h, slot, base, g, s_ref, x_ref):
        keys = kbuf[h, slot]
        for u in range(2):
            s = nt_dot(keys, qx[base + g * 2 + u])
            s_ref[u] = s
            x_ref[u] = jnp.max(s, axis=0, keepdims=True) * SCALE

    def update(j, s, top, vt):
        before = m_ref[j]
        now = jnp.maximum(before, top)
        p = jnp.exp2(s * SCALE - now)
        fade = jnp.exp2(before - now)
        l_ref[j] = l_ref[j] * fade + jnp.sum(p, axis=0, keepdims=True)
        m_ref[j] = now
        hi, lo = split(p)
        acc_ref[j] = acc_ref[j] * fade + (dot(vt, hi) + dot(vt, lo))

    def absorb(h, slot, base, g, s_ref, x_ref):
        for u in range(2):
            update(base + g * 2 + u, s_ref[u], x_ref[u], vbuf[h, slot])

    def flash_block(h, slot, base):
        def score_one(g):
            s = nt_dot(kbuf[h, slot], qx[base + g])
            s_ref, x_ref = (s_a, x_a) if g % 4 < 2 else (s_b, x_b)
            s_ref[g % 2] = s
            x_ref[g % 2] = jnp.max(s, axis=0, keepdims=True) * SCALE

        def absorb_one(g):
            s_ref, x_ref = (s_a, x_a) if g % 4 < 2 else (s_b, x_b)
            update(base + g, s_ref[g % 2], x_ref[g % 2], vbuf[h, slot])

        for g in range(3):
            score_one(g)
        for g in range(8):
            absorb_one(g)
            if g + 3 < 8:
                score_one(g + 3)

    def pick_slot_share():
        for cp in dq_copies + scat_copies:
            cp.wait_send()
        for i in range(3):
            src = (t + 3 - i) % 4
            remote(cand.at[0], scat.at[src], scat_send.at[i], scat_recv.at[src], tp_peer[i]).wait_recv()
        source = my_head // 2
        for i in range(2):
            quarter = scat[0, i]
            for q in range(1, 4):
                quarter = jnp.where(source == q, scat[q, i], quarter)
            slot_rows[me, 64 * i : 64 * i + 64, :] = quarter
        send_share(slot_share)

    def stretch_part():
        take_share(stretch_share)
        for h in range(2):
            kst[h] = share[:, h * 32 : (h + 1) * 32, :].reshape(ROWS, HEAD)
            vst[h] = share[:, 64 + h * 32 : 96 + h * 32, :].reshape(ROWS, HEAD).T
        kk = lax.broadcasted_iota(jnp.int32, (ROWS, ROWS), 0)
        key_row = (kk // 32) * ROWS + d * 32 + kk % 32
        query_row = c * ROWS + lax.broadcasted_iota(jnp.int32, (ROWS, ROWS), 1)
        usable = key_row <= query_row

        def stretch_score(h, g, s_ref, x_ref):
            for u in range(2):
                s = jnp.where(usable, nt_dot(kst[h], qx[h * 8 + g * 2 + u, :, :HEAD]), NEG)
                s_ref[u, :ROWS] = s
                x_ref[u] = jnp.max(s, axis=0, keepdims=True) * SCALE

        def stretch_absorb(h, g, s_ref, x_ref):
            for u in range(2):
                update(h * 8 + g * 2 + u, s_ref[u, :ROWS], x_ref[u], vst[h])

        def body(h, carry):
            stretch_score(h, 0, s_a, x_a)
            stretch_score(h, 1, s_b, x_b)
            stretch_absorb(h, 0, s_a, x_a)
            stretch_score(h, 2, s_a, x_a)
            stretch_absorb(h, 1, s_b, x_b)
            stretch_score(h, 3, s_b, x_b)
            stretch_absorb(h, 2, s_a, x_a)
            stretch_absorb(h, 3, s_b, x_b)
            return carry

        lax.fori_loop(0, 2, body, 0)

    def decode_cache():
        for cp in cache_copies:
            cp.wait()
        step_row = lax.broadcasted_iota(jnp.int32, (16, 1), 0) >= 8
        for r in range(4):
            qf = dq_rows[pl.ds(r, 16, stride=4), :]
            s = nt_dot(qf.astype(BF), ck[r]) * SCALE
            s = jnp.where(lax.broadcasted_iota(jnp.int32, (16, CACHE), 1) < lengths_ref[r], s, NEG)
            new = []
            for u in range(2):
                sn = jnp.sum(qf * dk_ref[u].astype(F32)[r : r + 1, :], axis=1, keepdims=True) * SCALE
                new.append(jnp.where(step_row, sn, NEG) if u else sn)
            top = jnp.maximum(jnp.max(s, axis=1, keepdims=True), jnp.maximum(new[0], new[1]))
            p = jnp.exp2(s - top)
            pn = [jnp.exp2(sn - top) for sn in new]
            total = jnp.sum(p, axis=1, keepdims=True) + pn[0] + pn[1]
            hi, lo = split(p)
            mixed = dot(jnp.concatenate([hi, lo], axis=0), cv[r])
            mixed = mixed[:16] + mixed[16:]
            for u in range(2):
                mixed = mixed + pn[u] * dv_ref[u].astype(F32)[r : r + 1, :]
            dec_o[pl.ds(r, 16, stride=4), :] = mixed / total
            dec_l[pl.ds(r, 16, stride=4), :] = jnp.broadcast_to(top + jnp.log2(total), (16, HEAD))

    dret_copies = [
        remote(dres.at[(t + 1 + i) % 4], dret.at[t], dret_send.at[i], dret_recv.at[t], tp_peer[i]) for i in range(3)
    ]

    def decode_stretch():
        take_share(slot_share)
        vslot[...] = slot_rows[:, 64:128, :].reshape(BLOCK, HEAD).T
        for i in range(3):
            src = (t + 3 - i) % 4
            remote(dqall.at[src], dqall.at[src], dq_send.at[i], dq_recv.at[src], tp_peer[i]).wait_recv()
        keys = slot_rows[:, 0:64, :].reshape(BLOCK, HEAD)
        s = nt_dot(keys, dqall[...].reshape(4 * 64, HEAD)) * SCALE
        top = jnp.max(s, axis=0, keepdims=True)
        p = jnp.exp2(s - top)
        total = jnp.sum(p, axis=0, keepdims=True)
        hi, lo = split(p)
        o = ((dot(vslot[...], hi) + dot(vslot[...], lo)) / total).T
        lse = jnp.broadcast_to(top + jnp.log2(total), (HEAD, 256)).T
        for q in range(4):
            dres[q, 0] = o[q * 64 : (q + 1) * 64]
            dres[q, 1] = lse[q * 64 : (q + 1) * 64]
        dret[t] = dres[t]
        for cp in dret_copies:
            cp.start()

    def decode_finish():
        for i in range(3):
            src = (t + 3 - i) % 4
            remote(dres.at[0], dret.at[src], dret_send.at[i], dret_recv.at[src], tp_peer[i]).wait_recv()
        top = dec_l[...]
        for q in range(4):
            top = jnp.maximum(top, dret[q, 1])
        w = jnp.exp2(dec_l[...] - top)
        num, den = w * dec_o[...], w
        for q in range(4):
            w = jnp.exp2(dret[q, 1] - top)
            num, den = num + w * dret[q, 0], den + w
        res = num / den
        for u in range(2):
            for g in range(GROUP):
                at = (u * GROUP + g) * 4
                dec_ref[u, :, g * HEAD : (g + 1) * HEAD] = res[at : at + 4, :].astype(BF)

    def core_copy(h):
        return remote(obuf.at[h, 1 - co], cbuf.at[h], core_send.at[h], core_recv.at[h], core_peer)

    def y_copy(h, i):
        return remote(
            obuf.at[h, co, (y + 1 + i) % 4], ybuf.at[h, y], y_send.at[h, i], y_recv.at[h, y], y_peer[i]
        )

    def finish_head(h):
        def body(g, carry):
            j = h * 8 + g
            o = (acc_ref[j] * (1.0 / l_ref[j])).T
            for k in range(8):
                obuf[h, k % 2, k // 2, g] = o[k * 32 : (k + 1) * 32]
            return carry

        lax.fori_loop(0, 8, body, 0, unroll=4)
        lse = [m_ref[h * 8 + g] + jnp.log2(l_ref[h * 8 + g]) for g in range(8)]
        lse = jnp.concatenate(lse + [jnp.zeros((120, ROWS), F32)], axis=0).T
        for k in range(8):
            obuf[h, k % 2, k // 2, 8] = lse[k * 32 : (k + 1) * 32]
        core_copy(h).start()

    def merge_cores(h):
        core_copy(h).wait_recv()

        def body(i, carry):
            a, b = obuf[h, co, i, 8], cbuf[h, i, 8]
            top = jnp.maximum(a, b)
            wa, wb = jnp.exp2(a - top), jnp.exp2(b - top)
            both = wa + wb
            obuf[h, co, i, 8] = top + jnp.log2(both)
            wa, wb = wa / both, wb / both
            for g in range(8):
                obuf[h, co, i, g] = obuf[h, co, i, g] * wa[:, g : g + 1] + cbuf[h, i, g] * wb[:, g : g + 1]
            return carry

        lax.fori_loop(0, 4, body, 0, unroll=2)
        for i in range(3):
            y_copy(h, i).start()

    def merge_y(h):
        for i in range(3):
            src = (y + 3 - i) % 4
            remote(
                obuf.at[h, co, 0], ybuf.at[h, src], y_send.at[h, i], y_recv.at[h, src], y_peer[i]
            ).wait_recv()
        ybuf[h, y] = obuf[h, co, y]
        parts = [ybuf.at[h, i] for i in range(4)]
        if h == 1:
            back_copy.wait_recv()
            parts.append(zbuf.at[1])
        lse = [p[8] for p in parts]
        top = functools.reduce(jnp.maximum, lse)
        w = [jnp.exp2(a - top) for a in lse]
        total = functools.reduce(jnp.add, w)
        inv = 1.0 / total
        w = [a * inv for a in w]
        if h == 2:
            zbuf[0, 8] = top + jnp.log2(total)
        for g in range(8):
            o = functools.reduce(jnp.add, [p[g] * a[:, g : g + 1] for p, a in zip(parts, w)])
            if h == 2:
                zbuf[0, g] = o
                continue
            out_ref[:, (h * 8 + g) * HEAD : (h * 8 + g + 1) * HEAD] = o.astype(BF)

    back_copy = remote(zbuf.at[0], zbuf.at[1], back_sem.at[0], back_sem.at[1], dev[Z])

    def send_back():
        merge_y(2)
        back_copy.start()

    ahead = {k: [] for k in range(16)}
    ahead[2] += [lambda: arrive(1, L), lambda: arrive(1, R), spread_queries]
    ahead[4] += [lambda: arrive(0, L), lambda: arrive(0, R), take_queries]
    ahead[5] += [lambda: arrive_one(0, Z, 0)]
    ahead[6] += [lambda: arrive_one(0, Z, 1), lambda: pass_share(stretch_share), pick_slot_share]
    ahead[7] += [lambda: arrive(1, O)]
    ahead[9] += [lambda: finish_head(2)]
    ahead[10] += [lambda: merge_cores(2)]
    ahead[11] += [lambda: arrive(0, ZL), lambda: arrive(0, ZR), lambda: arrive(0, O), stretch_part, lambda: finish_head(1)]
    ahead[12] += [lambda: merge_cores(1), lambda: pass_share(slot_share)]
    ahead[14] += [send_back]
    ahead[15] += [lambda: arrive(0, ZO)]

    def step(n, carry):
        h = 0
        slot = 0
        base = 0
        for k, (hk, which, rows) in enumerate(ORDER):
            if hk:
                h = h + jnp.where(n == k, 1, 0)
                base = base + jnp.where(n == k, 16 if rows == PAIR else 8, 0)
            slot = slot + jnp.where(n == k, slots[which], 0)
            if ahead[k]:

                def go(k=k):
                    for f in ahead[k]:
                        f()

                pl.when(n == k)(go)
        flash_block(h, slot, base)
        return carry

    lax.fori_loop(0, 16, step, 0)
    finish_head(0)
    decode_stretch()
    merge_cores(0)
    decode_cache()
    merge_y(1)
    decode_finish()
    merge_y(0)

    pair_copy.wait_send()
    back_copy.wait_send()
    for i in range(7):
        q_copy(i).wait_send()
    for h, sends in ((0, pair_sends), (0, x_sends), (1, x_sends)):
        for s in sends:
            make(h, s).wait_send()
    for which, sends in forwards.items():
        for h in range(2 if which in (L, R) else 1):
            for s in sends:
                make(h, s).wait_send()
    share_done(stretch_share)
    share_done(slot_share)
    for cp in dret_copies:
        cp.wait_send()
    for h in range(3):
        core_copy(h).wait_send()
        for i in range(3):
            y_copy(h, i).wait_send()


def fused(blocks, args):
    vmem = pl.BlockSpec(memory_space=pltpu.VMEM)
    smem = pl.BlockSpec(memory_space=pltpu.SMEM)
    anym = pl.BlockSpec(memory_space=pl.ANY)
    dma = pltpu.SemaphoreType.DMA
    return pl.pallas_call(
        functools.partial(kernel, blocks),
        out_shape=(
            jax.ShapeDtypeStruct((32, 2048), BF),
            jax.ShapeDtypeStruct((2, 4, GROUP * HEAD), BF),
        ),
        in_specs=[smem] * 3 + [vmem] * 8 + [anym] * 2,
        out_specs=(vmem, vmem),
        scratch_shapes=[
            pltpu.VMEM((4, CACHE, HEAD), BF),
            pltpu.VMEM((4, CACHE, HEAD), BF),
            pltpu.VMEM((24, ROWS, 2 * HEAD), BF),
            pltpu.VMEM((2, 8, BLOCK, 2 * HEAD), BF),
            pltpu.VMEM((2, 8, HEAD, BLOCK), BF),
            pltpu.VMEM((32, 8 * HEAD), BF),
            pltpu.VMEM((8, 32, 8 * HEAD), BF),
            pltpu.VMEM((8, 128, HEAD), BF),
            pltpu.VMEM((8, 128, HEAD), BF),
            pltpu.VMEM((4, 2, 64, HEAD), BF),
            pltpu.VMEM((4, 2, 64, HEAD), BF),
            pltpu.VMEM((64, HEAD), F32),
            pltpu.VMEM((4, 64, HEAD), BF),
            pltpu.VMEM((2, ROWS, HEAD), BF),
            pltpu.VMEM((2, HEAD, ROWS), BF),
            pltpu.VMEM((HEAD, BLOCK), BF),
            pltpu.VMEM((4, 2, 64, HEAD), F32),
            pltpu.VMEM((4, 2, 64, HEAD), F32),
            pltpu.VMEM((64, HEAD), F32),
            pltpu.VMEM((64, HEAD), F32),
            pltpu.VMEM((2, BLOCK, ROWS), F32),
            pltpu.VMEM((2, BLOCK, ROWS), F32),
            pltpu.VMEM((2, 1, ROWS), F32),
            pltpu.VMEM((2, 1, ROWS), F32),
            pltpu.VMEM((24, 1, ROWS), F32),
            pltpu.VMEM((24, 1, ROWS), F32),
            pltpu.VMEM((24, HEAD, ROWS), F32),
            pltpu.VMEM((3, 2, 4, 9, 32, HEAD), F32),
            pltpu.VMEM((3, 4, 9, 32, HEAD), F32),
            pltpu.VMEM((3, 4, 9, 32, HEAD), F32),
            pltpu.VMEM((2, 9, 32, HEAD), F32),
            dma((4, 2)),
            dma((2, 14)),
            dma((2, 8, 2)),
            dma((7,)),
            dma((8,)),
            dma((7,)),
            dma((8,)),
            dma((3,)),
            dma((4,)),
            dma((3,)),
            dma((4,)),
            dma((3,)),
            dma((4,)),
            dma((3,)),
            dma((3,)),
            dma((3, 3)),
            dma((3, 4)),
            dma((2,)),
            dma((7,)),
            dma((8,)),
            dma((2,)),
        ],
        compiler_params=pltpu.CompilerParams(
            collective_id=blocks, has_side_effects=True, vmem_limit_bytes=56 << 20
        ),
        name=f"attention_{blocks}",
    )(*args)


def shards(
    stretch_query_rows,
    stretch_key_rows,
    stretch_value_rows,
    prefix_key_rows,
    prefix_value_rows,
    offset,
    decode_query_rows,
    decode_keys,
    decode_value_rows,
    cache_keys,
    cached_value_rows,
    cache_lengths,
    head_slot_index,
):
    args = (
        offset,
        head_slot_index,
        cache_lengths,
        stretch_query_rows,
        prefix_key_rows,
        prefix_value_rows,
        stretch_key_rows,
        stretch_value_rows,
        decode_query_rows.reshape(2, 4, GROUP * HEAD),
        decode_keys.reshape(2, 4, HEAD),
        decode_value_rows.reshape(2, 4, HEAD),
        cache_keys.reshape(4, CACHE, HEAD),
        cached_value_rows.reshape(4, CACHE, HEAD),
    )
    prefill_out, dec = fused(8, args)
    return prefill_out, dec.reshape(2, 4, 1, GROUP * HEAD)


def solution(mesh):
    placed = (
        P("ctx", "tp"),
        P("ctx", "tp"),
        P("ctx", "tp"),
        P(("ctx", "dec"), "tp"),
        P(("ctx", "dec"), "tp"),
        P(),
        P(None, ("ctx", "tp"), "dec", None),
        P(None, ("ctx", "tp"), "dec", None),
        P(None, ("ctx", "tp"), "dec", None),
        P(("ctx", "tp"), "dec", None, None),
        P(("ctx", "tp"), "dec", None, None),
        P(("ctx", "tp")),
        P(),
    )
    return jax.shard_map(
        shards,
        mesh=mesh,
        in_specs=placed,
        out_specs=(P(("ctx", "dec"), "tp"), P(None, ("ctx", "tp"), "dec", None)),
        check_vma=False,
    )
```
